512 devices in a mesh: lon: 64 (over z_lo, y, core), lat: 8 (over z_hi, x).
Axes of the slice: x: 4, y: 4, z: 16 (z_hi: 2, z_lo: 8; z = z_hi * 8 + z_lo), core: 2. Of those that a mesh axis runs over, the one named last changes fastest.
Arguments:
- fields: bfloat16 [2, 48, 768, 192], P(None, 'lat', 'lon'), may hold values from -20 to 20
- cotangent: bfloat16 [2, 48, 768, 192], P(None, 'lat', 'lon'), may hold values from -6 to 6
- norm_gains: float32 [2, 192], replicated, may hold values from 0.1 to 1.9
- w_qkv: bfloat16 [2, 192, 576], replicated, may hold values from -0.4375 to 0.4375
- w_proj: bfloat16 [2, 192, 192], replicated, may hold values from -0.4375 to 0.4375
- tables: float32 [2, 8, 6, 3312], P(None, 'lat'), may hold values from -4 to 400
Outputs:
- block_out: bfloat16 [2, 48, 768, 192], P(None, 'lat', 'lon')
- grad_field: bfloat16 [2, 48, 768, 192], P(None, 'lat', 'lon')
- grad_gains: float32 [2, 192], replicated
- grad_qkv: float32 [2, 192, 576], replicated
- grad_proj: float32 [2, 192, 192], replicated
- grad_tables: float32 [2, 8, 6, 3312], P(None, 'lat')
The draws below stay inside these ranges and needn't reach their ends.
All inputs are finite; a program needn't handle non-finite values.
Results may differ from the reference program's by a relative error of at most 0.013.
Values may be sent and summed in bfloat16 or wider, within the bound.
A program may use at most 64 MiB of HBM per device.

```python
import jax
import jax.numpy as jnp
from jax import lax

C = 192
HEADS = 6
WLEV = 2
WLAT = 6
WLON = 12
WIN = 144
TAB = 3312
LEV = 2
NLAT = 48
NLON = 768
LATW = 8


def draw_fields(key, part):
    key = jax.random.fold_in(key, 11)
    array_shape = (LEV, NLAT, NLON, C)
    return jnp.clip(jax.random.normal(key, array_shape, jnp.float32), -6.0, 6.0).astype(jnp.bfloat16)


def draw_tables(key, part):
    key = jax.random.fold_in(key, 23)
    array_shape = (2, LATW, HEADS, TAB)
    return jnp.clip(jax.random.normal(key, array_shape, jnp.float32), -4.0, 4.0)


def block_scale(own_key, dims, cuts, smallest, top_value):
    level, own = 1.0, jax.random.fold_in(own_key, 6)
    for dim, blocks in cuts:
        steps = jnp.exp(jax.random.uniform(jax.random.fold_in(own, dim), (blocks,), jnp.float32, smallest / len(cuts), top_value / len(cuts)))
        level = level * jnp.repeat(steps, dims[dim] // blocks).reshape([-1 if axis == dim else 1 for axis in range(len(dims))])
    return level


def noise(rng, extent, spread, most, cuts=(), held_as=jnp.bfloat16):
    factor_of = block_scale(rng, extent, cuts, -0.22, 0.18) if cuts else 1.0
    entries = jax.random.normal(rng, extent, jnp.float32) * spread * factor_of
    return jnp.minimum(jnp.maximum(entries, -most), most).astype(held_as)


def setup_inputs(seed: int = 0) -> dict:
    key_of = jax.random.split(jax.random.key(seed), 7)
    return {
        "fields": draw_fields(jax.random.fold_in(key_of[6], 71), 0),
        "cotangent": noise(key_of[1], (LEV, NLAT, NLON, C), 1.0, 6.0, ((1, 8), (2, 64))),
        "norm_gains": jnp.clip(1.0 + 0.18 * jax.random.normal(key_of[2], (2, C), jnp.float32), 0.1, 1.9),
        "w_qkv": noise(key_of[3], (2, C, 3 * C), C ** -0.5, 0.4375),
        "w_proj": noise(key_of[4], (2, C, C), C ** -0.5, 0.4375),
        "tables": draw_tables(jax.random.fold_in(key_of[6], 71), 0),
    }


epsilon = 1e-05
highest = lax.Precision.HIGHEST

def to_windows(grid_in):
    levels, lat_rows, lon_cols, channels = grid_in.shape
    blocks = grid_in.reshape(levels, lat_rows // WLAT, WLAT, lon_cols // WLON, WLON, channels)
    blocks = blocks.transpose(1, 3, 0, 2, 4, 5)
    return blocks.reshape(lat_rows // WLAT, lon_cols // WLON, levels * WLAT * WLON, channels)

def from_windows(windowed, levels, lat_rows, lon_cols):
    channels = windowed.shape[-1]
    blocks = windowed.reshape(lat_rows // WLAT, lon_cols // WLON, levels, WLAT, WLON, channels)
    blocks = blocks.transpose(2, 0, 3, 1, 4, 5)
    return blocks.reshape(levels, lat_rows, lon_cols, channels)

def level_windows(windowed, levels):
    lat_types, lon_wins, tokens, channels = windowed.shape
    per_level = tokens // levels
    shaped = windowed.reshape(lat_types, lon_wins, levels // WLEV, WLEV * per_level, channels)
    return shaped.reshape(lat_types, lon_wins * (levels // WLEV), WLEV * per_level, channels)

def level_unwindows(windowed, levels):
    lat_types, wins, win_tokens, channels = windowed.shape
    return windowed.reshape(lat_types, wins // (levels // WLEV), levels // WLEV * win_tokens, channels)

def offset_table():
    offset_span = 2 * WLON - 1
    query_lon = jnp.arange(WLON)[:, None]
    key_lon = jnp.arange(WLON)[None, :]
    offsets = (key_lon - query_lon + WLON - 1)[:, :, None]
    return (jnp.arange(offset_span)[None, None, :] == offsets).astype(jnp.float32)

def expand_bias(table):
    type_count, head_count = (table.shape[0], table.shape[1])
    shaped = table.reshape(type_count, head_count, WLEV, WLEV, WLAT, WLAT, 2 * WLON - 1)
    full_bias = jnp.einsum('thabcdr,qkr->thacqbdk', shaped, offset_table(), precision=highest)
    return full_bias.reshape(type_count, head_count, WIN, WIN)

def reduce_bias(full_grad):
    type_count, head_count = (full_grad.shape[0], full_grad.shape[1])
    shaped = full_grad.reshape(type_count, head_count, WLEV, WLAT, WLON, WLEV, WLAT, WLON)
    table = jnp.einsum('thacqbdk,qkr->thabcdr', shaped, offset_table(), precision=highest)
    return table.reshape(type_count, head_count, TAB)

def region_ids(levels, lat_pos, lat_total, lon_cols):
    level_pos = jnp.arange(levels).astype(jnp.int32)
    level_part = (level_pos >= levels - WLEV).astype(jnp.int32) + (level_pos >= levels - WLEV // 2).astype(jnp.int32)
    lat_part = (lat_pos >= lat_total - WLAT).astype(jnp.int32) + (lat_pos >= lat_total - WLAT // 2).astype(jnp.int32)
    labels = level_part[:, None] * 3 + lat_part[None, :]
    labels = jnp.broadcast_to(labels[:, :, None, None], (levels, lat_pos.shape[0], lon_cols, 1))
    return level_windows(to_windows(labels), levels)[..., 0]

def rounded(values):
    return lax.optimization_barrier(values.astype(jnp.bfloat16)).astype(jnp.float32)

def split_heads(win_qkv, head_count):
    win_count, win_size, qkv_width = win_qkv.shape
    head_dim = qkv_width // (3 * head_count)
    return win_qkv.reshape(win_count, win_size, 3, head_count, head_dim).astype(jnp.float32)

def attn_probs(pieces, bias, labels):
    score_scale = pieces.shape[-1] ** (-0.5)
    scores = jnp.einsum('oqhe,okhe->ohqk', pieces[:, :, 0], pieces[:, :, 1]) * score_scale + bias[None]
    if labels is not None:
        allowed = labels[:, None, :, None] == labels[:, None, None, :]
        scores = jnp.where(allowed, scores, -1e+30)
    row_max = lax.optimization_barrier(jnp.max(scores, axis=-1, keepdims=True))
    exp_scores = jnp.exp(scores - row_max)
    return exp_scores / lax.optimization_barrier(jnp.sum(exp_scores, axis=-1, keepdims=True))

def attention_forward(win_qkv, bias, labels):
    pieces = split_heads(win_qkv, bias.shape[0])
    probs_round = rounded(attn_probs(pieces, bias, labels))
    mixed_out = jnp.einsum('ohqk,okhe->oqhe', probs_round, pieces[:, :, 2])
    return mixed_out.reshape(win_qkv.shape[0], win_qkv.shape[1], -1)

def attention_backward(win_qkv, bias, labels, grad_mixed):
    win_count, win_size = (win_qkv.shape[0], win_qkv.shape[1])
    pieces = split_heads(win_qkv, bias.shape[0])
    head_count, head_dim = (pieces.shape[3], pieces.shape[4])
    score_scale = head_dim ** (-0.5)
    attn_p = attn_probs(pieces, bias, labels)
    grad_heads = grad_mixed.reshape(win_count, win_size, head_count, head_dim).astype(jnp.float32)
    grad_probs = jnp.einsum('oqhe,okhe->ohqk', grad_heads, pieces[:, :, 2])
    grad_scores = attn_p * (grad_probs - lax.optimization_barrier(jnp.sum(attn_p * grad_probs, axis=-1, keepdims=True)))
    bias_grad = lax.optimization_barrier(jnp.sum(grad_scores, axis=0))
    scores_round = rounded(grad_scores)
    grad_query = jnp.einsum('ohqk,okhe->oqhe', scores_round, pieces[:, :, 1]) * score_scale
    grad_key = jnp.einsum('ohqk,oqhe->okhe', scores_round, pieces[:, :, 0]) * score_scale
    grad_value = jnp.einsum('ohqk,oqhe->okhe', rounded(attn_p), grad_heads)
    grad_win = jnp.stack([grad_query, grad_key, grad_value], axis=2).astype(jnp.bfloat16)
    return (grad_win.reshape(win_count, win_size, -1), bias_grad)

def attend_types(win_qkv, bias_full, labels):
    if labels is None:
        return lax.map(lambda grouped: attention_forward(grouped[0], grouped[1], None), (win_qkv, bias_full))
    return lax.map(lambda grouped: attention_forward(grouped[0], grouped[1], grouped[2]), (win_qkv, bias_full, labels))

def backward_types(win_qkv, bias_full, labels, grad_windows):
    if labels is None:
        return lax.map(lambda grouped: attention_backward(grouped[0], grouped[1], None, grouped[2]), (win_qkv, bias_full, grad_windows))
    return lax.map(lambda grouped: attention_backward(grouped[0], grouped[1], grouped[2], grouped[3]), (win_qkv, bias_full, labels, grad_windows))

def block_forward(grid_in, gain_vec, weight_qkv, weight_proj, bias_full, labels):
    levels, lat_rows, lon_cols, channels = grid_in.shape
    flat_rows = grid_in.reshape(-1, channels).astype(jnp.float32)
    centred = flat_rows - lax.optimization_barrier(jnp.mean(flat_rows, axis=-1, keepdims=True))
    inv_std = lax.rsqrt(lax.optimization_barrier(jnp.mean(centred * centred, axis=-1, keepdims=True)) + epsilon)
    normed = centred * inv_std
    normed_b = (normed * gain_vec).astype(jnp.bfloat16)
    qkv_rows = jnp.dot(normed_b, weight_qkv, preferred_element_type=jnp.float32).astype(jnp.bfloat16)
    win_qkv = level_windows(to_windows(qkv_rows.reshape(levels, lat_rows, lon_cols, 3 * channels)), levels)
    mixed_out = attend_types(win_qkv, bias_full, labels).astype(jnp.bfloat16)
    merged = from_windows(level_unwindows(mixed_out, levels), levels, lat_rows, lon_cols).reshape(-1, channels)
    block_rows = flat_rows + jnp.dot(merged, weight_proj, preferred_element_type=jnp.float32)
    return (block_rows.astype(jnp.bfloat16).reshape(grid_in.shape), (normed, inv_std, normed_b, win_qkv, merged))

def block_backward(saved, grad_out, gain_vec, weight_qkv, weight_proj, bias_full, labels):
    normed, inv_std, normed_b, win_qkv, merged = saved
    levels, lat_rows, lon_cols, channels = grad_out.shape
    grad_rows = grad_out.reshape(-1, channels)
    proj_sum = jnp.dot(merged.T, grad_rows, preferred_element_type=jnp.float32)
    grad_merged = jnp.dot(grad_rows, weight_proj.T, preferred_element_type=jnp.float32).astype(jnp.bfloat16)
    grad_windows = level_windows(to_windows(grad_merged.reshape(levels, lat_rows, lon_cols, channels)), levels)
    grad_win_qkv, bias_sum = backward_types(win_qkv, bias_full, labels, grad_windows)
    grad_qkv_rows = from_windows(level_unwindows(grad_win_qkv, levels), levels, lat_rows, lon_cols).reshape(-1, 3 * channels)
    qkv_sum = jnp.dot(normed_b.T, grad_qkv_rows, preferred_element_type=jnp.float32)
    grad_normed = jnp.dot(grad_qkv_rows, weight_qkv.T, preferred_element_type=jnp.float32)
    gain_sum = lax.optimization_barrier(jnp.sum(grad_normed * normed, axis=0))
    grad_scaled = grad_normed * gain_vec
    grad_centre = grad_scaled - lax.optimization_barrier(jnp.mean(grad_scaled, axis=-1, keepdims=True))
    grad_centre = grad_centre - normed * lax.optimization_barrier(jnp.mean(grad_scaled * normed, axis=-1, keepdims=True))
    grad_in = (grad_rows.astype(jnp.float32) + inv_std * grad_centre).astype(jnp.bfloat16)
    return (grad_in.reshape(grad_out.shape), gain_sum, qkv_sum, proj_sum, reduce_bias(bias_sum))

def reference(fields, cotangent, norm_gains, w_qkv, w_proj, tables):
    levels, lat_total, lon_total, channels = fields.shape
    labels = region_ids(levels, jnp.arange(lat_total).astype(jnp.int32), lat_total, lon_total)
    bias_first = expand_bias(tables[0])
    bias_second = expand_bias(tables[1])
    shift_minus = (-(WLEV // 2), -(WLAT // 2), -(WLON // 2))
    shift_plus = (WLEV // 2, WLAT // 2, WLON // 2)
    first_out, saved_first = block_forward(fields, norm_gains[0], w_qkv[0], w_proj[0], bias_first, None)
    shifted = jnp.roll(first_out, shift_minus, (0, 1, 2))
    second_out, saved_second = block_forward(shifted, norm_gains[1], w_qkv[1], w_proj[1], bias_second, labels)
    block_out = jnp.roll(second_out, shift_plus, (0, 1, 2))
    grad_second = jnp.roll(cotangent, shift_minus, (0, 1, 2))
    grad_shifted, gain_two, qkv_two, proj_two, table_two = block_backward(saved_second, grad_second, norm_gains[1], w_qkv[1], w_proj[1], bias_second, labels)
    grad_first = jnp.roll(grad_shifted, shift_plus, (0, 1, 2))
    grad_field, gain_one, qkv_one, proj_one, table_one = block_backward(saved_first, grad_first, norm_gains[0], w_qkv[0], w_proj[0], bias_first, None)
    token_scale = float(levels * lat_total * lon_total) ** (-0.5)
    window_scale = float(lon_total // WLON) ** (-0.5)
    grad_gains = jnp.stack([gain_one, gain_two]) * token_scale
    grad_qkv = jnp.stack([qkv_one, qkv_two]) * token_scale
    grad_proj = jnp.stack([proj_one, proj_two]) * token_scale
    grad_tables = jnp.stack([table_one, table_two]) * window_scale
    return (block_out, grad_field, grad_gains, grad_qkv, grad_proj, grad_tables)
```

```python
import functools

import jax
import jax.numpy as jnp
from jax import lax
from jax.experimental import pallas as pl
from jax.experimental.pallas import tpu as pltpu
from jax.sharding import PartitionSpec as P

MESH = pl.DeviceIdType.MESH
ROWS = 192
QUAD = 48
C = 192
HEADS = 6
HD = 32
LAGS = 276
SCALE = HD**-0.5
epsilon = 1e-05
f32, bf16 = jnp.float32, jnp.bfloat16


def mm(a, b):
    return lax.dot_general(a, b, (((1,), (0,)), ((), ())), preferred_element_type=f32)


def mm_nt(a, b):
    return lax.dot_general(a, b, (((1,), (1,)), ((), ())), preferred_element_type=f32)


def mm_tn(a, b):
    return lax.dot_general(a, b, (((0,), (0,)), ((), ())), preferred_element_type=f32)


def row_parts(row):
    half = (row >= 96).astype(jnp.int32)
    lon = (row >> 3) - 12 * half
    slot = row & 7
    level = (slot >= 3).astype(jnp.int32)
    return half, lon, slot, level, slot - 3 * level


def iota(shape, dim):
    return lax.broadcasted_iota(jnp.int32, shape, dim)


def to_rows_matrix():
    half, lon, slot, level, lat = row_parts(iota((ROWS, 1), 0))
    source = (level * 6 + half * 3 + lat) * 16 + lon
    source = jnp.where(slot < 6, source, -1)
    return (iota((ROWS, ROWS), 1) == source).astype(f32).astype(bf16)


def from_rows_matrix():
    half, lon, slot, level, lat = row_parts(iota((1, ROWS), 1))
    target = (level * 6 + half * 3 + lat) * 16 + lon
    target = jnp.where(slot < 6, target, -1)
    return (iota((ROWS, ROWS), 0) == target).astype(f32).astype(bf16)


def load_grid(ref):
    grid = ref[...].astype(f32)
    grid = jnp.concatenate([grid, jnp.zeros((2, 6, 4, C), f32)], axis=2)
    return grid.reshape(ROWS, C).astype(bf16)


def store_grid(ref, rows):
    grid = rows.reshape(2, 6, 16, C)
    ref[...] = grid[:, :, :12, :].astype(bf16)


def build_lags(lag_ref):
    half, lon, slot, level, lat = row_parts(iota((ROWS, 1), 0))
    start = (level * 6 + half * 3 + lat) * 23 + lon + 11
    start = jnp.where(slot < 6, start, -100)
    lane = iota((ROWS, LAGS), 1)
    for o in range(12):
        lag_ref[o] = (lane == start - o).astype(f32).astype(bf16)


def expand(table, lag_ref, bias_ref, block, last):
    high = table.astype(bf16)
    rest = table - high.astype(f32)
    middle = rest.astype(bf16)
    low = (rest - middle.astype(f32)).astype(bf16)
    stacked = jnp.concatenate([high, middle, low], axis=0)
    khalf, _, kslot, klevel, _ = row_parts(iota((1, ROWS), 1))
    key_ok = kslot < 6
    if block:
        row = iota((96, 1), 0)
        slot = row & 7
        qhalf = (row >> 3) & 1
        qlevel = (slot >= 3).astype(jnp.int32)
        same_half = jnp.broadcast_to(qhalf, (96, ROWS)) == jnp.broadcast_to(khalf, (96, ROWS))
        same_level = jnp.broadcast_to(qlevel, (96, ROWS)) == jnp.broadcast_to(klevel, (96, ROWS))
        key_ok = key_ok & same_level & (same_half | jnp.logical_not(last))
    for o in range(12):
        parts = mm_nt(stacked, lag_ref[o])
        full = (parts[:96] + parts[96:192]) + parts[192:]
        full = jnp.where(key_ok, full, -1e30)
        bias_ref[block, :, :, o] = full.reshape(HEADS, 2, 8, ROWS)


def reduce_lags(gs_ref, lag_ref):
    total = jnp.zeros((96, LAGS), f32)
    for o in range(12):
        part = gs_ref[:, :, o].reshape(96, ROWS).astype(bf16)
        total = total + mm(part, lag_ref[o])
    return total


def head_mask(head):
    lane = iota((ROWS, C), 1)
    return (lane >= head * HD) & (lane < (head + 1) * HD)


def only(head, values):
    return jnp.where(head_mask(head), values, jnp.zeros_like(values))


def forward(block, rows_f, gain, w_qkv, w_proj, bias_ref, p_ref):
    centred = rows_f - jnp.mean(rows_f, axis=-1, keepdims=True)
    inv_std = lax.rsqrt(jnp.mean(centred * centred, axis=-1, keepdims=True) + epsilon)
    normed = centred * inv_std
    normed_b = (normed * gain).astype(bf16)
    q = mm(normed_b, w_qkv[:, :C]).astype(bf16)
    k = mm(normed_b, w_qkv[:, C : 2 * C]).astype(bf16)
    v = mm(normed_b, w_qkv[:, 2 * C :]).astype(bf16)
    mixed = jnp.zeros((ROWS, C), f32)
    for head in range(HEADS):
        bias = bias_ref[block, head].reshape(ROWS, ROWS)
        scores = mm_nt(only(head, q), k) * SCALE + bias
        exp_scores = jnp.exp(scores - jnp.max(scores, axis=-1, keepdims=True))
        probs = exp_scores / jnp.sum(exp_scores, axis=-1, keepdims=True)
        p_ref[block, head] = probs
        mixed = jnp.where(head_mask(head), mm(probs.astype(bf16), v), mixed)
    mixed_b = mixed.astype(bf16)
    result = rows_f + mm(mixed_b, w_proj)
    return result, (normed, inv_std, normed_b, q, k, v, mixed_b)


def backward(block, saved, grad_b, gain, w_qkv, w_proj, p_ref, gs_ref):
    normed, inv_std, normed_b, q, k, v, mixed_b = saved
    proj_sum = mm_tn(mixed_b, grad_b)
    grad_mixed = mm_nt(grad_b, w_proj).astype(bf16)
    grad_q = jnp.zeros((ROWS, C), f32)
    grad_k = jnp.zeros((ROWS, C), f32)
    grad_v = jnp.zeros((ROWS, C), f32)
    for head in range(HEADS):
        probs = p_ref[block, head]
        grad_head = only(head, grad_mixed)
        grad_probs = mm_nt(grad_head, v)
        weighted = jnp.sum(probs * grad_probs, axis=-1, keepdims=True)
        grad_scores = probs * (grad_probs - weighted)
        gs_ref[head] = grad_scores.reshape(2, 12, 8, ROWS)
        scores_b = grad_scores.astype(bf16)
        grad_q = jnp.where(head_mask(head), mm(scores_b, k), grad_q)
        grad_k = grad_k + mm_tn(scores_b, only(head, q))
        grad_v = grad_v + mm_tn(probs.astype(bf16), grad_head)
    grad_q = (grad_q * SCALE).astype(bf16)
    grad_k = (grad_k * SCALE).astype(bf16)
    grad_v = grad_v.astype(bf16)
    sums = jnp.concatenate(
        [mm_tn(normed_b, grad_q), mm_tn(normed_b, grad_k), mm_tn(normed_b, grad_v), proj_sum], axis=1
    )
    grad_normed = mm_nt(grad_q, w_qkv[:, :C]) + mm_nt(grad_k, w_qkv[:, C : 2 * C])
    grad_normed = grad_normed + mm_nt(grad_v, w_qkv[:, 2 * C :])
    gain_sum = jnp.sum(grad_normed * normed, axis=0, keepdims=True)
    grad_scaled = grad_normed * gain
    grad_centre = grad_scaled - jnp.mean(grad_scaled, axis=-1, keepdims=True)
    grad_centre = grad_centre - normed * jnp.mean(grad_scaled * normed, axis=-1, keepdims=True)
    grad_in = (grad_b.astype(f32) + inv_std * grad_centre).astype(bf16)
    return grad_in, gain_sum, sums


def place():
    lon, lat = lax.axis_index("lon"), lax.axis_index("lat")
    return dict(core=lon % 2, y=(lon // 2) % 4, z=(lat // 4) * 8 + lon // 8, x=lat % 4, lon=lon, lat=lat)


def device(core, y, z, x):
    return {"lon": ((z % 8) * 4 + y) * 2 + core, "lat": (z // 8) * 4 + x}


XY = [(dx, dy) for dx in range(4) for dy in range(4) if (dx, dy) != (0, 0)]


class Halo:
    def __init__(self, src, dst, send, recv, towards, sizes):
        self.src, self.dst, self.send, self.recv, self.towards = src, dst, send, recv, towards
        self.sizes = sizes

    def copies(self):
        me = place()
        n_lon, n_lat = self.sizes
        found = []
        for slot, (half, lon_half) in enumerate([(0, 0), (0, 1), (1, 0)]):
            if self.towards < 0:
                lat = (me["lat"] - (1 - half) + n_lat) % n_lat
                lon = (me["lon"] - (1 - lon_half) + n_lon) % n_lon
                source = (half, lon_half)
            else:
                lat = (me["lat"] + half_of(half)) % n_lat
                lon = (me["lon"] + half_of(lon_half)) % n_lon
                source = (1 - half, 1 - lon_half)
            start = source[0] * 96 + source[1] * QUAD
            end = (1 - source[0]) * 96 + (1 - source[1]) * QUAD
            found.append(
                pltpu.make_async_remote_copy(
                    src_ref=self.src.at[pl.ds(start, QUAD)],
                    dst_ref=self.dst.at[pl.ds(end, QUAD)],
                    send_sem=self.send.at[slot],
                    recv_sem=self.recv.at[slot],
                    device_id={"lon": lon, "lat": lat},
                    device_id_type=MESH,
                )
            )
        return found

    def start(self):
        for copy in self.copies():
            copy.start()
        own = 96 + QUAD if self.towards < 0 else 0
        there = 0 if self.towards < 0 else 96 + QUAD
        self.dst[there : there + QUAD] = self.src[own : own + QUAD]

    def finish(self):
        for copy in self.copies():
            copy.wait_recv()

    def drain(self):
        for copy in self.copies():
            copy.wait_send()


def half_of(half):
    return 1 - half


class Sums:
    def __init__(self, refs, send, recv):
        (self.w_src, self.t_src, self.w_core, self.t_core, self.w_xy, self.t_y, self.w_z, self.t_z,
         self.w_all, self.t_all) = refs
        self.send, self.recv = send, recv
        self.me = place()

    def copy(self, step, src, dst, to):
        copy = pltpu.make_async_remote_copy(
            src_ref=src, dst_ref=dst, send_sem=self.send.at[step], recv_sem=self.recv.at[step],
            device_id=to, device_id_type=MESH,
        )
        copy.start()

    def total(self, step):
        return {
            0: self.w_core, 1: self.t_core, 2: self.w_xy, 3: self.t_y, 4: self.w_xy, 5: self.t_z.at[pl.ds(0, 7)],
            6: self.w_xy, 7: self.t_y, 8: self.w_core, 9: self.t_core,
        }[step]

    def wait(self, step):
        pltpu.make_async_copy(self.total(step), self.total(step), self.recv.at[step]).wait()

    def drain(self):
        for step in range(10):
            pltpu.make_async_copy(self.total(step), self.total(step), self.send.at[step]).wait()

    def fill(self, sums, gains, table):
        for half in range(2):
            for tile in range(3):
                lanes = sums[:, (half * 3 + tile) * 128 : (half * 3 + tile + 1) * 128]
                self.w_src[half, 4 * tile : 4 * tile + 4] = lanes.reshape(4, 48, 128).astype(bf16)
            self.w_src[half, 12:16] = jnp.zeros((4, 48, 128), bf16)
        gains = jnp.concatenate([gains, jnp.zeros((1, 64), f32)], axis=1)
        gains = jnp.concatenate([gains[:, :128], gains[:, 128:], jnp.zeros((46, 128), f32)], axis=0)
        self.w_src[0, 12] = gains.astype(bf16)
        table = jnp.concatenate([table, jnp.zeros((96, 512 - LAGS), f32)], axis=1)
        for half in range(2):
            for tile in range(2):
                lanes = table[:, (half * 2 + tile) * 128 : (half * 2 + tile + 1) * 128]
                self.t_src[half, 2 * tile : 2 * tile + 2] = lanes.reshape(2, 48, 128).astype(bf16)

    def core_start(self):
        me = self.me
        other = 1 - me["core"]
        to = device(other, me["y"], me["z"], me["x"])
        self.copy(0, self.w_src.at[other], self.w_core, to)
        self.copy(1, self.t_src.at[other], self.t_core, to)

    def core_finish(self):
        me = self.me
        self.wait(0)
        self.w_core[...] = (self.w_src[me["core"]].astype(f32) + self.w_core[...].astype(f32)).astype(bf16)
        self.wait(1)
        self.t_core[...] = (self.t_src[me["core"]].astype(f32) + self.t_core[...].astype(f32)).astype(bf16)

    def xy_start(self):
        me = self.me
        for slot, (dx, dy) in enumerate(XY):
            x, y = (me["x"] + dx) % 4, (me["y"] + dy) % 4
            self.copy(2, self.w_core.at[y * 4 + x], self.w_xy.at[slot], device(me["core"], y, me["z"], x))
        for slot in range(3):
            y = (me["y"] + slot + 1) % 4
            self.copy(3, self.t_core.at[y], self.t_y.at[slot], device(me["core"], y, me["z"], me["x"]))

    def xy_finish(self):
        me = self.me
        self.wait(2)
        total = self.w_core[me["y"] * 4 + me["x"]].astype(f32)
        for slot in range(15):
            total = total + self.w_xy[slot].astype(f32)
        self.w_z[me["z"]] = total.astype(bf16)
        self.wait(3)
        total = self.t_core[me["y"]].astype(f32)
        for slot in range(3):
            total = total + self.t_y[slot].astype(f32)
        self.t_z[me["z"] % 8] = total.astype(bf16)

    def z_start(self):
        me = self.me
        for dz in (8, 7, 9, 6, 10, 5, 11, 4, 12, 3, 13, 2, 14, 1, 15):
            to = device(me["core"], me["y"], (me["z"] + dz) % 16, me["x"])
            self.copy(4, self.w_z.at[me["z"]], self.w_z.at[me["z"]], to)
        low = me["z"] % 8
        for dz in range(1, 8):
            to = device(me["core"], me["y"], me["z"] - low + (low + dz) % 8, me["x"])
            self.copy(5, self.t_z.at[low], self.t_z.at[low], to)

    def z_finish(self):
        me = self.me
        self.wait(4)
        total = self.w_z[0].astype(f32)
        for slot in range(1, 16):
            total = total + self.w_z[slot].astype(f32)
        self.w_all[me["core"], me["y"] * 4 + me["x"]] = total.astype(bf16)
        self.wait(5)
        total = self.t_z[0].astype(f32)
        for slot in range(1, 8):
            total = total + self.t_z[slot].astype(f32)
        self.t_all[me["core"], me["y"]] = total.astype(bf16)

    def back_start(self):
        me = self.me
        at = me["y"] * 4 + me["x"]
        for dx, dy in XY:
            to = device(me["core"], (me["y"] + dy) % 4, me["z"], (me["x"] + dx) % 4)
            self.copy(6, self.w_all.at[me["core"], at], self.w_all.at[me["core"], at], to)
        for dy in range(1, 4):
            to = device(me["core"], (me["y"] + dy) % 4, me["z"], me["x"])
            self.copy(7, self.t_all.at[me["core"], me["y"]], self.t_all.at[me["core"], me["y"]], to)

    def back_finish(self):
        self.wait(6)
        self.wait(7)

    def pair_start(self):
        me = self.me
        to = device(1 - me["core"], me["y"], me["z"], me["x"])
        self.copy(8, self.w_all.at[me["core"]], self.w_all.at[me["core"]], to)
        self.copy(9, self.t_all.at[me["core"]], self.t_all.at[me["core"]], to)

    def pair_finish(self, block, scale, table_scale, gains_ref, qkv_ref, proj_ref, table_ref):
        self.wait(8)
        self.wait(9)
        tiles = []
        for half in range(2):
            for tile in range(3):
                part = self.w_all[half, 4 * tile : 4 * tile + 4].astype(f32)
                tiles.append(part.reshape(ROWS, 128) * scale)
        for tile in range(4):
            qkv_ref[block, :, tile * 128 : (tile + 1) * 128] = tiles[tile]
        qkv_ref[block, :, 512:576] = tiles[4][:, :64]
        proj_ref[block] = jnp.concatenate([tiles[4][:, 64:], tiles[5]], axis=1)
        gains = self.w_all[0, 12].astype(f32) * scale
        gains_ref[block : block + 1, :128] = gains[0:1]
        gains_ref[block : block + 1, 128:] = gains[1:2, :64]
        for tile in range(3):
            part = self.t_all[tile // 2, 2 * (tile % 2) : 2 * (tile % 2) + 2].astype(f32)
            table_ref[block, :, tile * 128 : (tile + 1) * 128] = part.reshape(96, 128) * table_scale


def kernel(sizes, scale, table_scale, x_ref, ct_ref, gain_ref, w_qkv_ref, w_proj_ref, table_ref,
           out_ref, field_ref, gains_ref, qkv_ref, proj_ref, tables_ref,
           lag_ref, bias_ref, p_ref, gs_ref, halo_src, halo_dst, halo_send, halo_recv, *sum_refs):
    n_lon, n_lat = sizes
    alone = n_lon * n_lat == 1
    me = place()
    if not alone:
        barrier = pltpu.get_barrier_semaphore()
        count = 0
        for dlat, dlon in ((0, 1), (1, 0), (1, 1)):
            for sign in (1, -1):
                to = {"lon": (me["lon"] + sign * dlon + n_lon) % n_lon, "lat": (me["lat"] + sign * dlat + n_lat) % n_lat}
                pl.semaphore_signal(barrier, inc=1, device_id=to, device_id_type=MESH)
                count += 1
        partners = [device(1 - me["core"], me["y"], me["z"], me["x"])]
        partners += [device(me["core"], (me["y"] + dy) % 4, me["z"], (me["x"] + dx) % 4) for dx, dy in XY]
        partners += [device(me["core"], me["y"], (me["z"] + dz) % 16, me["x"]) for dz in range(1, 16)]
        for to in partners:
            pl.semaphore_signal(barrier, inc=1, device_id=to, device_id_type=MESH)
        count += len(partners)
    halos = [
        Halo(halo_src.at[n], halo_dst.at[n], halo_send.at[n], halo_recv.at[n], -1 if n < 2 else 1, sizes)
        for n in range(4)
    ]
    first, turned, second, back = halos

    def exchange(halo, rows):
        halo.src[...] = rows
        if alone:
            for half in range(2):
                for lon_half in range(2):
                    start = half * 96 + lon_half * QUAD
                    end = (1 - half) * 96 + (1 - lon_half) * QUAD
                    halo.dst[end : end + QUAD] = halo.src[start : start + QUAD]
        else:
            halo.start()

    def arrived(halo):
        if not alone:
            halo.finish()
        return halo.dst[...]

    last = me["lat"] == n_lat - 1
    to_rows = to_rows_matrix()
    from_rows = from_rows_matrix()
    x_rows = mm(to_rows, load_grid(x_ref))
    ct_rows = mm(to_rows, load_grid(ct_ref)).astype(bf16)
    build_lags(lag_ref)
    expand(table_ref[0], lag_ref, bias_ref, 0, last)
    gain = [gain_ref[0:1], gain_ref[1:2]]
    w_qkv = [w_qkv_ref[0], w_qkv_ref[1]]
    w_proj = [w_proj_ref[0], w_proj_ref[1]]
    first_out, saved_first = forward(0, x_rows, gain[0], w_qkv[0], w_proj[0], bias_ref, p_ref)
    if not alone:
        pl.semaphore_wait(barrier, count)
    exchange(first, first_out.astype(bf16))
    exchange(turned, ct_rows)
    expand(table_ref[1], lag_ref, bias_ref, 1, last)
    shifted = arrived(first).astype(f32)
    second_out, saved_second = forward(1, shifted, gain[1], w_qkv[1], w_proj[1], bias_ref, p_ref)
    exchange(second, second_out.astype(bf16))
    grad_second = arrived(turned)
    grad_shifted, gain_two, sums_two = backward(1, saved_second, grad_second, gain[1], w_qkv[1], w_proj[1], p_ref, gs_ref)
    exchange(back, grad_shifted)
    table_two = reduce_lags(gs_ref, lag_ref)
    if alone:
        grad_first = arrived(back)
        grad_field, gain_one, sums_one = backward(0, saved_first, grad_first, gain[0], w_qkv[0], w_proj[0], p_ref, gs_ref)
        table_one = reduce_lags(gs_ref, lag_ref)
        for block, (gains, sums, table) in enumerate(((gain_one, sums_one, table_one), (gain_two, sums_two, table_two))):
            gains_ref[block : block + 1] = gains * scale
            qkv_ref[block] = sums[:, :576] * scale
            proj_ref[block] = sums[:, 576:] * scale
            tables_ref[block, :, :LAGS] = table * table_scale
    else:
        outputs = (scale, table_scale, gains_ref, qkv_ref, proj_ref, tables_ref)
        half = len(sum_refs) // 2
        two = Sums(sum_refs[: half - 2], *sum_refs[half - 2 : half])
        one = Sums(sum_refs[half : 2 * half - 2], *sum_refs[2 * half - 2 :])
        two.fill(sums_two, gain_two, table_two)
        two.core_start()
        two.core_finish()
        two.xy_start()
        grad_first = arrived(back)
        grad_field, gain_one, sums_one = backward(0, saved_first, grad_first, gain[0], w_qkv[0], w_proj[0], p_ref, gs_ref)
        table_one = reduce_lags(gs_ref, lag_ref)
        one.fill(sums_one, gain_one, table_one)
        one.core_start()
        two.xy_finish()
        two.z_start()
        one.core_finish()
        one.xy_start()
    store_grid(field_ref, mm(from_rows, grad_field))
    store_grid(out_ref, mm(from_rows, arrived(second)))
    if not alone:
        one.xy_finish()
        one.z_start()
        two.z_finish()
        two.back_start()
        two.back_finish()
        two.pair_start()
        one.z_finish()
        one.back_start()
        two.pair_finish(1, *outputs)
        one.back_finish()
        one.pair_start()
        for halo in halos:
            halo.drain()
        two.drain()
        one.pair_finish(0, *outputs)
        one.drain()


def arrange(tables):
    shaped = tables[:, 0].reshape(2, HEADS, 2, 2, 2, 3, 6, 23)
    shaped = jnp.stack([shaped[0], shaped[1][:, ::-1, ::-1]])
    shaped = shaped.transpose(0, 1, 4, 2, 5, 3, 6, 7).reshape(2, HEADS * 2, 6, LAGS)
    return jnp.pad(shaped, ((0, 0), (0, 0), (0, 2), (0, 0))).reshape(2, 96, LAGS)


def restore(lagged):
    shaped = lagged[:, :, :LAGS].reshape(2, HEADS * 2, 8, LAGS)[:, :, :6]
    shaped = shaped.reshape(2, HEADS, 2, 2, 3, 2, 6, 23).transpose(0, 1, 3, 5, 2, 4, 6, 7)
    shaped = jnp.stack([shaped[0], shaped[1][:, ::-1, ::-1]])
    return shaped.reshape(2, 1, HEADS, 3312)


def per_device(fields, cotangent, norm_gains, w_qkv, w_proj, tables, *, sizes, interpret=False):
    n_lon, n_lat = sizes
    scale = float(2 * 6 * n_lat * 12 * n_lon) ** -0.5
    table_scale = float(n_lon) ** -0.5
    shapes = [
        jax.ShapeDtypeStruct(fields.shape, bf16),
        jax.ShapeDtypeStruct(fields.shape, bf16),
        jax.ShapeDtypeStruct((2, C), f32),
        jax.ShapeDtypeStruct((2, C, 3 * C), f32),
        jax.ShapeDtypeStruct((2, C, C), f32),
        jax.ShapeDtypeStruct((2, 96, 384), f32),
    ]
    vmem = pl.BlockSpec(memory_space=pltpu.VMEM)
    sum_scratch = [
        pltpu.VMEM((2, 16, 48, 128), bf16),
        pltpu.VMEM((2, 4, 48, 128), bf16),
        pltpu.VMEM((16, 48, 128), bf16),
        pltpu.VMEM((4, 48, 128), bf16),
        pltpu.VMEM((15, 48, 128), bf16),
        pltpu.VMEM((3, 48, 128), bf16),
        pltpu.VMEM((16, 48, 128), bf16),
        pltpu.VMEM((8, 48, 128), bf16),
        pltpu.VMEM((2, 16, 48, 128), bf16),
        pltpu.VMEM((2, 4, 48, 128), bf16),
        pltpu.SemaphoreType.DMA((10,)),
        pltpu.SemaphoreType.DMA((10,)),
    ]
    outs = pl.pallas_call(
        functools.partial(kernel, sizes, scale, table_scale),
        out_shape=shapes,
        in_specs=[vmem] * 6,
        out_specs=[vmem] * 6,
        scratch_shapes=[
            pltpu.VMEM((12, ROWS, LAGS), bf16),
            pltpu.VMEM((2, HEADS, 2, 12, 8, ROWS), f32),
            pltpu.VMEM((2, HEADS, ROWS, ROWS), f32),
            pltpu.VMEM((HEADS, 2, 12, 8, ROWS), f32),
            pltpu.VMEM((4, ROWS, C), bf16),
            pltpu.VMEM((4, ROWS, C), bf16),
            pltpu.SemaphoreType.DMA((4, 3)),
            pltpu.SemaphoreType.DMA((4, 3)),
        ]
        + (sum_scratch * 2 if n_lon * n_lat > 1 else []),
        compiler_params=pltpu.CompilerParams(
            collective_id=0 if n_lon * n_lat > 1 else None, has_side_effects=True, vmem_limit_bytes=56 * 2**20
        ),
        interpret=interpret,
    )(fields, cotangent, norm_gains, w_qkv, w_proj, arrange(tables))
    return (*outs[:5], restore(outs[5]))


def solution(mesh):
    grid = P(None, "lat", "lon", None)
    bands = P(None, "lat", None, None)
    sizes = (mesh.shape["lon"], mesh.shape["lat"])
    return jax.shard_map(
        functools.partial(per_device, sizes=sizes),
        mesh=mesh,
        in_specs=(grid, grid, P(), P(), P(), bands),
        out_specs=(grid, grid, P(), P(), P(), bands),
        check_vma=False,
    )
```

```python
import functools

import jax
import jax.numpy as jnp
from jax import lax
from jax.experimental import pallas as pl
from jax.experimental.pallas import tpu as pltpu
from jax.sharding import PartitionSpec as P

MESH = pl.DeviceIdType.MESH
ROWS = 192
WIN = 144
QUAD = 48
C = 192
HEADS = 6
HD = 32
LAGS = 276
TAB = 3312
SCALE = HD**-0.5
epsilon = 1e-05
f32, bf16 = jnp.float32, jnp.bfloat16


def mm(a, b):
    return lax.dot_general(a, b, (((1,), (0,)), ((), ())), preferred_element_type=f32)


def mm_nt(a, b):
    return lax.dot_general(a, b, (((1,), (1,)), ((), ())), preferred_element_type=f32)


def mm_tn(a, b):
    return lax.dot_general(a, b, (((0,), (0,)), ((), ())), preferred_element_type=f32)


def row_parts(row):
    half = (row >= 96).astype(jnp.int32)
    lon = (row >> 3) - 12 * half
    slot = row & 7
    level = (slot >= 3).astype(jnp.int32)
    return half, lon, slot, level, slot - 3 * level


def iota(shape, dim):
    return lax.broadcasted_iota(jnp.int32, shape, dim)


def to_rows_matrix():
    half, lon, slot, level, lat = row_parts(iota((ROWS, 1), 0))
    source = ((half * 3 + lat) * 12 + lon) * 2 + level
    source = jnp.where(slot < 6, source, -1)
    return (iota((ROWS, WIN), 1) == source).astype(f32).astype(bf16)


def from_rows_matrix():
    half, lon, slot, level, lat = row_parts(iota((1, ROWS), 1))
    target = ((half * 3 + lat) * 12 + lon) * 2 + level
    target = jnp.where(slot < 6, target, -1)
    return (iota((WIN, ROWS), 0) == target).astype(f32).astype(bf16)


def load_grid(ref):
    return ref[...].reshape(WIN, C)


def store_grid(ref, rows):
    ref[...] = rows.astype(bf16).reshape(6, 12, 2, C)


def build_lags(lag_ref):
    half, lon, slot, level, lat = row_parts(iota((ROWS, 1), 0))
    start = (level * 6 + half * 3 + lat) * 23 + lon + 11
    start = jnp.where(slot < 6, start, -100)
    lane = iota((ROWS, LAGS), 1)
    for o in range(12):
        lag_ref[o] = (lane == start - o).astype(f32).astype(bf16)


def table_places(block):
    for half in range(2):
        for slot in range(6):
            level, lat = slot // 3, 3 * half + slot % 3
            levels = [(level, 0), (level, 1)] if block == 0 else [(1 - level, 1), (1 - level, 0)]
            yield half, slot, [((a * 2 + b) * 6 + lat) * 138 for a, b in levels]


def expand(table_ref, flat_ref, lag_ref, bias_ref, block, last):
    flat = table_ref[block].reshape(HEADS, TAB)
    flat_ref[...] = jnp.zeros_like(flat_ref)
    for half, slot, starts in table_places(block):
        pieces = [flat[:, start : start + 138] for start in starts]
        flat_ref[:, half, slot, :] = jnp.concatenate(pieces, axis=1)
    table = flat_ref[...].reshape(96, LAGS)
    high = table.astype(bf16)
    rest = table - high.astype(f32)
    middle = rest.astype(bf16)
    low = (rest - middle.astype(f32)).astype(bf16)
    stacked = jnp.concatenate([high, middle, low], axis=0)
    khalf, _, kslot, klevel, _ = row_parts(iota((1, ROWS), 1))
    key_ok = kslot < 6
    if block:
        row = iota((96, 1), 0)
        slot = row & 7
        qhalf = (row >> 3) & 1
        qlevel = (slot >= 3).astype(jnp.int32)
        same_half = jnp.broadcast_to(qhalf, (96, ROWS)) == jnp.broadcast_to(khalf, (96, ROWS))
        same_level = jnp.broadcast_to(qlevel, (96, ROWS)) == jnp.broadcast_to(klevel, (96, ROWS))
        key_ok = key_ok & same_level & (same_half | jnp.logical_not(last))
    for o in range(12):
        parts = mm_nt(stacked, lag_ref[o])
        full = (parts[:96] + parts[96:192]) + parts[192:]
        full = jnp.where(key_ok, full, -1e30)
        bias_ref[block, :, :, o] = full.reshape(HEADS, 2, 8, ROWS)


def reduce_lags(gs_ref, lag_ref):
    total = jnp.zeros((96, LAGS), f32)
    for o in range(12):
        part = gs_ref[:, :, o].reshape(96, ROWS).astype(bf16)
        total = total + mm(part, lag_ref[o])
    return total


def dense_rows():
    row = iota((1, 96), 1)
    slot = row & 7
    target = (((row >> 3) & 1) * 6 + slot) * 6 + (row >> 4)
    target = jnp.where(slot < 6, target, -1)
    return (iota((80, 96), 0) == target).astype(f32).astype(bf16)


def head_mask(head):
    lane = iota((ROWS, C), 1)
    return (lane >= head * HD) & (lane < (head + 1) * HD)


def only(head, values):
    return jnp.where(head_mask(head), values, jnp.zeros_like(values))


def forward(block, rows_f, gain, w_qkv, w_proj, bias_ref, p_ref):
    centred = rows_f - jnp.mean(rows_f, axis=-1, keepdims=True)
    inv_std = lax.rsqrt(jnp.mean(centred * centred, axis=-1, keepdims=True) + epsilon)
    normed = centred * inv_std
    normed_b = (normed * gain).astype(bf16)
    q = mm(normed_b, w_qkv[:, :C]).astype(bf16)
    k = mm(normed_b, w_qkv[:, C : 2 * C]).astype(bf16)
    v = mm(normed_b, w_qkv[:, 2 * C :]).astype(bf16)
    mixed = jnp.zeros((ROWS, C), f32)
    for head in range(HEADS):
        bias = bias_ref[block, head].reshape(ROWS, ROWS)
        scores = mm_nt(only(head, q), k) * SCALE + bias
        exp_scores = jnp.exp(scores - jnp.max(scores, axis=-1, keepdims=True))
        probs = exp_scores / jnp.sum(exp_scores, axis=-1, keepdims=True)
        p_ref[block, head] = probs
        mixed = jnp.where(head_mask(head), mm(probs.astype(bf16), v), mixed)
    mixed_b = mixed.astype(bf16)
    result = rows_f + mm(mixed_b, w_proj)
    return result, (normed, inv_std, normed_b, q, k, v, mixed_b)


def backward(block, saved, grad_b, gain, w_qkv, w_proj, p_ref, gs_ref):
    normed, inv_std, normed_b, q, k, v, mixed_b = saved
    proj_sum = mm_tn(mixed_b, grad_b)
    grad_mixed = mm_nt(grad_b, w_proj).astype(bf16)
    grad_q = jnp.zeros((ROWS, C), f32)
    grad_k = jnp.zeros((ROWS, C), f32)
    grad_v = jnp.zeros((ROWS, C), f32)
    for head in range(HEADS):
        probs = p_ref[block, head]
        grad_head = only(head, grad_mixed)
        grad_probs = mm_nt(grad_head, v)
        weighted = jnp.sum(probs * grad_probs, axis=-1, keepdims=True)
        grad_scores = probs * (grad_probs - weighted)
        gs_ref[head] = grad_scores.reshape(2, 12, 8, ROWS)
        scores_b = grad_scores.astype(bf16)
        grad_q = jnp.where(head_mask(head), mm(scores_b, k), grad_q)
        grad_k = grad_k + mm_tn(scores_b, only(head, q))
        grad_v = grad_v + mm_tn(probs.astype(bf16), grad_head)
    grad_q = (grad_q * SCALE).astype(bf16)
    grad_k = (grad_k * SCALE).astype(bf16)
    grad_v = grad_v.astype(bf16)
    sums = jnp.concatenate(
        [mm_tn(normed_b, grad_q), mm_tn(normed_b, grad_k), mm_tn(normed_b, grad_v), proj_sum], axis=1
    )
    grad_normed = mm_nt(grad_q, w_qkv[:, :C]) + mm_nt(grad_k, w_qkv[:, C : 2 * C])
    grad_normed = grad_normed + mm_nt(grad_v, w_qkv[:, 2 * C :])
    gain_sum = jnp.sum(grad_normed * normed, axis=0, keepdims=True)
    grad_scaled = grad_normed * gain
    grad_centre = grad_scaled - jnp.mean(grad_scaled, axis=-1, keepdims=True)
    grad_centre = grad_centre - normed * jnp.mean(grad_scaled * normed, axis=-1, keepdims=True)
    grad_in = (grad_b.astype(f32) + inv_std * grad_centre).astype(bf16)
    return grad_in, gain_sum, sums


def place():
    lon, lat = lax.axis_index("lon"), lax.axis_index("lat")
    return dict(core=lon % 2, y=(lon // 2) % 4, z=(lat // 4) * 8 + lon // 8, x=lat % 4, lon=lon, lat=lat)


def device(core, y, z, x):
    return {"lon": ((z % 8) * 4 + y) * 2 + core, "lat": (z // 8) * 4 + x}


XY = [(dx, dy) for dx in range(4) for dy in range(4) if (dx, dy) != (0, 0)]


class Halo:
    def __init__(self, src, dst, send, recv, towards, sizes):
        self.src, self.dst, self.send, self.recv, self.towards = src, dst, send, recv, towards
        self.sizes = sizes

    def copies(self):
        me = place()
        n_lon, n_lat = self.sizes
        found = []
        for slot, (half, lon_half) in enumerate([(0, 0), (0, 1), (1, 0)]):
            if self.towards < 0:
                lat = (me["lat"] - (1 - half) + n_lat) % n_lat
                lon = (me["lon"] - (1 - lon_half) + n_lon) % n_lon
                source = (half, lon_half)
            else:
                lat = (me["lat"] + half_of(half)) % n_lat
                lon = (me["lon"] + half_of(lon_half)) % n_lon
                source = (1 - half, 1 - lon_half)
            start = source[0] * 96 + source[1] * QUAD
            end = (1 - source[0]) * 96 + (1 - source[1]) * QUAD
            found.append(
                pltpu.make_async_remote_copy(
                    src_ref=self.src.at[pl.ds(start, QUAD)],
                    dst_ref=self.dst.at[pl.ds(end, QUAD)],
                    send_sem=self.send.at[slot],
                    recv_sem=self.recv.at[slot],
                    device_id={"lon": lon, "lat": lat},
                    device_id_type=MESH,
                )
            )
        return found

    def start(self):
        for copy in self.copies():
            copy.start()
        own = 96 + QUAD if self.towards < 0 else 0
        there = 0 if self.towards < 0 else 96 + QUAD
        self.dst[there : there + QUAD] = self.src[own : own + QUAD]

    def finish(self):
        for copy in self.copies():
            copy.wait_recv()

    def drain(self):
        for copy in self.copies():
            copy.wait_send()


def half_of(half):
    return 1 - half


PLANE = [(dx, dy, dc) for dx in (2, 1, 3, 0) for dy in (2, 1, 3, 0) for dc in (1, 0) if (dx, dy, dc) != (0, 0, 0)]
YC = [(dy, dc) for dy in (2, 1, 3, 0) for dc in (1, 0) if (dy, dc) != (0, 0)]
FAR = (8, 7, 9, 6, 10, 5, 11, 4, 12, 3, 13, 2, 14, 1, 15)


def piece(index, rows):
    return pl.ds(pl.multiple_of(index * rows, rows), rows)


class Sums:
    def __init__(self, refs, send, recv):
        self.w_src, self.t_src, self.w_in, self.t_in, self.w_z, self.t_z, self.w_all, self.t_all = refs
        self.send, self.recv = send, recv
        self.me = me = place()
        self.w_at = (me["y"] * 4 + me["x"]) * 2 + me["core"]
        self.t_at = me["y"] * 2 + me["core"]

    def copy(self, step, src, dst, to):
        pltpu.make_async_remote_copy(
            src_ref=src, dst_ref=dst, send_sem=self.send.at[step], recv_sem=self.recv.at[step],
            device_id=to, device_id_type=MESH,
        ).start()

    def total(self, step):
        return (self.w_in, self.t_in, self.w_z.at[pl.ds(0, 15)], self.t_z.at[pl.ds(0, 7)], self.w_in, self.t_in)[step]

    def wait(self, step):
        pltpu.make_async_copy(self.total(step), self.total(step), self.recv.at[step]).wait()

    def drain(self):
        for step in range(6):
            pltpu.make_async_copy(self.total(step), self.total(step), self.send.at[step]).wait()

    def fill(self, sums, gains):
        for tile in range(6):
            lanes = sums[:, tile * 128 : (tile + 1) * 128]
            self.w_src[4 * tile : 4 * tile + 4] = lanes.reshape(4, 48, 128).astype(bf16)
        self.w_src[24:32] = jnp.zeros((8, 48, 128), bf16)
        gains = jnp.concatenate([gains, jnp.zeros((1, 64), f32)], axis=1)
        gains = jnp.concatenate([gains[:, :128], gains[:, 128:], jnp.zeros((46, 128), f32)], axis=0)
        self.w_src[24] = gains.astype(bf16)

    def fill_table(self, table):
        table = jnp.concatenate([table, jnp.zeros((96, 384 - LAGS), f32)], axis=1)
        table = mm(dense_rows(), table.astype(bf16)).astype(bf16)
        for tile in range(3):
            self.t_src[80 * tile : 80 * tile + 80] = table[:, tile * 128 : (tile + 1) * 128]
        self.t_src[240:256] = jnp.zeros((16, 128), bf16)

    def plane(self, dx, dy, dc):
        me = self.me
        x, y, core = (me["x"] + dx) % 4, (me["y"] + dy) % 4, (me["core"] + dc) % 2
        return (y * 4 + x) * 2 + core, y * 2 + core, device(core, y, me["z"], x)

    def scatter(self):
        for slot, offset in enumerate(PLANE):
            at, _, to = self.plane(*offset)
            self.copy(0, self.w_src.at[at], self.w_in.at[slot], to)

    def scatter_table(self):
        for slot, offset in enumerate(YC):
            _, at, to = self.plane(0, *offset)
            self.copy(1, self.t_src.at[piece(at, 32)], self.t_in.at[slot], to)

    def scattered(self):
        self.wait(0)
        total = self.w_src[self.w_at].astype(f32)
        for slot in range(31):
            total = total + self.w_in[slot].astype(f32)
        self.w_z[self.me["z"]] = total.astype(bf16)

    def scattered_table(self):
        self.wait(1)
        total = self.t_src[piece(self.t_at, 32)].astype(f32)
        for slot in range(7):
            total = total + self.t_in[slot].astype(f32)
        self.t_z[self.me["z"] % 8] = total.astype(bf16)

    def exchange(self):
        me = self.me
        for dz in FAR:
            to = device(me["core"], me["y"], (me["z"] + dz) % 16, me["x"])
            self.copy(2, self.w_z.at[me["z"]], self.w_z.at[me["z"]], to)

    def exchange_table(self):
        me = self.me
        low = me["z"] % 8
        for dz in (4, 3, 5, 2, 6, 1, 7):
            to = device(me["core"], me["y"], me["z"] - low + (low + dz) % 8, me["x"])
            self.copy(3, self.t_z.at[low], self.t_z.at[low], to)

    def exchanged(self):
        self.wait(2)
        total = self.w_z[0].astype(f32)
        for slot in range(1, 16):
            total = total + self.w_z[slot].astype(f32)
        self.w_all[self.w_at] = total.astype(bf16)

    def exchanged_table(self):
        self.wait(3)
        total = self.t_z[0].astype(f32)
        for slot in range(1, 8):
            total = total + self.t_z[slot].astype(f32)
        self.t_all[piece(self.t_at, 32)] = total.astype(bf16)

    def gather(self):
        for offset in PLANE:
            self.copy(4, self.w_all.at[self.w_at], self.w_all.at[self.w_at], self.plane(*offset)[2])

    def gather_table(self):
        own = piece(self.t_at, 32)
        for offset in YC:
            self.copy(5, self.t_all.at[own], self.t_all.at[own], self.plane(0, *offset)[2])

    def gathered(self, w_ref, t_ref):
        self.wait(4)
        w_ref[...] = self.w_all[...]
        self.wait(5)
        t_ref[...] = self.t_all[...]


def finish(scale, table_scale, grid_a, grid_b, w_one, w_two, t_one, t_two,
           out_ref, field_ref, gains_ref, qkv_ref, proj_ref, table_ref, flat_ref):
    out_ref[...] = grid_a[...]
    field_ref[...] = grid_b[...]
    for block, (w_all, t_all) in enumerate(((w_one, t_one), (w_two, t_two))):
        tiles = [w_all[4 * tile : 4 * tile + 4].astype(f32).reshape(ROWS, 128) * scale for tile in range(6)]
        for tile in range(4):
            qkv_ref[block, :, tile * 128 : (tile + 1) * 128] = tiles[tile]
        qkv_ref[block, :, 512:576] = tiles[4][:, :64]
        proj_ref[block] = jnp.concatenate([tiles[4][:, 64:], tiles[5]], axis=1)
        gains = w_all[24].astype(f32) * scale
        gains_ref[block : block + 1, :128] = gains[0:1]
        gains_ref[block : block + 1, 128:] = gains[1:2, :64]
        parts = [t_all[80 * tile : 80 * tile + 80].astype(f32) for tile in range(3)]
        table = jnp.concatenate(parts, axis=1) * table_scale
        for half, slot, starts in table_places(block):
            row = (half * 6 + slot) * 6
            for index, start in enumerate(starts):
                flat_ref[:, start : start + 138] = table[row : row + 6, index * 138 : index * 138 + 138]
        table_ref[block] = flat_ref[...].reshape(HEADS, 1, TAB)


def kernel(sizes, x_ref, ct_ref, gain_ref, w_qkv_ref, w_proj_ref, table_ref,
           out_ref, field_ref, w_one, w_two, t_one, t_two,
           flat_ref, lag_ref, bias_ref, p_ref, gs_ref, halo_src, halo_dst, halo_send, halo_recv, *sum_refs):
    n_lon, n_lat = sizes
    alone = n_lon * n_lat == 1
    me = place()
    if not alone:
        barrier = pltpu.get_barrier_semaphore()
        count = 0
        for dlat, dlon in ((0, 1), (1, 0), (1, 1)):
            for sign in (1, -1):
                to = {"lon": (me["lon"] + sign * dlon + n_lon) % n_lon, "lat": (me["lat"] + sign * dlat + n_lat) % n_lat}
                pl.semaphore_signal(barrier, inc=1, device_id=to, device_id_type=MESH)
                count += 1
        partners = [device((me["core"] + dc) % 2, (me["y"] + dy) % 4, me["z"], (me["x"] + dx) % 4) for dx, dy, dc in PLANE]
        partners += [device(me["core"], me["y"], (me["z"] + dz) % 16, me["x"]) for dz in FAR]
        for to in partners:
            pl.semaphore_signal(barrier, inc=1, device_id=to, device_id_type=MESH)
        count += len(partners)
    halos = [
        Halo(halo_src.at[n], halo_dst.at[n], halo_send.at[n], halo_recv.at[n], -1 if n < 2 else 1, sizes)
        for n in range(4)
    ]
    first, turned, second, back = halos

    def exchange(halo, rows):
        halo.src[...] = rows
        if alone:
            for half in range(2):
                for lon_half in range(2):
                    start = half * 96 + lon_half * QUAD
                    end = (1 - half) * 96 + (1 - lon_half) * QUAD
                    halo.dst[end : end + QUAD] = halo.src[start : start + QUAD]
        else:
            halo.start()

    def arrived(halo):
        if not alone:
            halo.finish()
        return halo.dst[...]

    last = me["lat"] == n_lat - 1
    to_rows = to_rows_matrix()
    from_rows = from_rows_matrix()
    x_rows = mm(to_rows, load_grid(x_ref))
    ct_rows = mm(to_rows, load_grid(ct_ref)).astype(bf16)
    build_lags(lag_ref)
    expand(table_ref, flat_ref, lag_ref, bias_ref, 0, last)
    gain = [gain_ref[0:1], gain_ref[1:2]]
    w_qkv = [w_qkv_ref[0], w_qkv_ref[1]]
    w_proj = [w_proj_ref[0], w_proj_ref[1]]
    first_out, saved_first = forward(0, x_rows, gain[0], w_qkv[0], w_proj[0], bias_ref, p_ref)
    if not alone:
        pl.semaphore_wait(barrier, count)
    exchange(first, first_out.astype(bf16))
    exchange(turned, ct_rows)
    expand(table_ref, flat_ref, lag_ref, bias_ref, 1, last)
    shifted = arrived(first).astype(f32)
    second_out, saved_second = forward(1, shifted, gain[1], w_qkv[1], w_proj[1], bias_ref, p_ref)
    exchange(second, second_out.astype(bf16))
    grad_second = arrived(turned)
    grad_shifted, gain_two, sums_two = backward(1, saved_second, grad_second, gain[1], w_qkv[1], w_proj[1], p_ref, gs_ref)
    exchange(back, grad_shifted)
    half = len(sum_refs) // 2
    two = Sums(sum_refs[: half - 2], *sum_refs[half - 2 : half])
    one = Sums(sum_refs[half : 2 * half - 2], *sum_refs[2 * half - 2 :])
    two.fill(sums_two, gain_two)
    if not alone:
        two.scatter()
    two.fill_table(reduce_lags(gs_ref, lag_ref))
    if not alone:
        two.scatter_table()
    grad_first = arrived(back)
    grad_field, gain_one, sums_one = backward(0, saved_first, grad_first, gain[0], w_qkv[0], w_proj[0], p_ref, gs_ref)
    one.fill(sums_one, gain_one)
    if alone:
        one.fill_table(reduce_lags(gs_ref, lag_ref))
        for sums, w_ref, t_ref in ((one, w_one, t_one), (two, w_two, t_two)):
            w_ref[...] = sums.w_src[...]
            t_ref[...] = sums.t_src[...]
    else:
        one.scatter()
        two.scattered()
        two.exchange()
        two.scattered_table()
        two.exchange_table()
        one.fill_table(reduce_lags(gs_ref, lag_ref))
        one.scatter_table()
    store_grid(field_ref, mm(from_rows, grad_field))
    store_grid(out_ref, mm(from_rows, arrived(second)))
    if not alone:
        one.scattered()
        one.exchange()
        one.scattered_table()
        one.exchange_table()
        two.exchanged()
        two.gather()
        two.exchanged_table()
        two.gather_table()
        for halo in halos:
            halo.drain()
        one.exchanged()
        one.gather()
        one.exchanged_table()
        one.gather_table()
        two.gathered(w_two, t_two)
        two.drain()
        one.gathered(w_one, t_one)
        one.drain()


def per_device(fields, cotangent, norm_gains, w_qkv, w_proj, tables, *, sizes, interpret=False):
    n_lon, n_lat = sizes
    scale = float(2 * 6 * n_lat * 12 * n_lon) ** -0.5
    table_scale = float(n_lon) ** -0.5
    vmem = pl.BlockSpec(memory_space=pltpu.VMEM)
    grid = jax.ShapeDtypeStruct((6, 12, 2, C), bf16)
    w_shape, t_shape = (32, 48, 128), (256, 128)
    many = n_lon * n_lat > 1
    sum_scratch = [
        pltpu.VMEM(w_shape, bf16),
        pltpu.VMEM(t_shape, bf16),
        pltpu.VMEM((31, 48, 128), bf16),
        pltpu.VMEM((7, 32, 128), bf16),
        pltpu.VMEM((16, 48, 128), bf16),
        pltpu.VMEM((8, 32, 128), bf16),
        pltpu.VMEM(w_shape, bf16),
        pltpu.VMEM(t_shape, bf16),
        pltpu.SemaphoreType.DMA((6,)),
        pltpu.SemaphoreType.DMA((6,)),
    ]
    found = pl.pallas_call(
        functools.partial(kernel, sizes),
        out_shape=[grid, grid] + [jax.ShapeDtypeStruct(w_shape, bf16)] * 2 + [jax.ShapeDtypeStruct(t_shape, bf16)] * 2,
        in_specs=[vmem] * 6,
        out_specs=[vmem] * 6,
        scratch_shapes=[
            pltpu.VMEM((HEADS, 2, 8, LAGS), f32),
            pltpu.VMEM((12, ROWS, LAGS), bf16),
            pltpu.VMEM((2, HEADS, 2, 12, 8, ROWS), f32),
            pltpu.VMEM((2, HEADS, ROWS, ROWS), f32),
            pltpu.VMEM((HEADS, 2, 12, 8, ROWS), f32),
            pltpu.VMEM((4, ROWS, C), bf16),
            pltpu.VMEM((4, ROWS, C), bf16),
            pltpu.SemaphoreType.DMA((4, 3)),
            pltpu.SemaphoreType.DMA((4, 3)),
        ]
        + sum_scratch * 2,
        compiler_params=pltpu.CompilerParams(
            collective_id=0 if many else None, has_side_effects=True, vmem_limit_bytes=56 * 2**20
        ),
        interpret=interpret,
    )(
        fields.transpose(1, 2, 0, 3),
        cotangent.transpose(1, 2, 0, 3),
        norm_gains,
        w_qkv,
        w_proj,
        tables.transpose(0, 2, 1, 3),
    )
    outs = pl.pallas_call(
        functools.partial(finish, scale, table_scale),
        out_shape=[
            grid,
            grid,
            jax.ShapeDtypeStruct((2, C), f32),
            jax.ShapeDtypeStruct((2, C, 3 * C), f32),
            jax.ShapeDtypeStruct((2, C, C), f32),
            jax.ShapeDtypeStruct((2, HEADS, 1, TAB), f32),
        ],
        in_specs=[vmem] * 6,
        out_specs=[vmem] * 6,
        scratch_shapes=[pltpu.VMEM((HEADS, TAB), f32)],
        compiler_params=pltpu.CompilerParams(vmem_limit_bytes=32 * 2**20),
        interpret=interpret,
    )(*found)
    grids = [rows.transpose(2, 0, 1, 3) for rows in outs[:2]]
    return (*grids, *outs[2:5], outs[5].transpose(0, 2, 1, 3))


def solution(mesh):
    grid = P(None, "lat", "lon", None)
    bands = P(None, "lat", None, None)
    sizes = (mesh.shape["lon"], mesh.shape["lat"])
    return jax.shard_map(
        functools.partial(per_device, sizes=sizes),
        mesh=mesh,
        in_specs=(grid, grid, P(), P(), P(), bands),
        out_specs=(grid, grid, P(), P(), P(), bands),
        check_vma=False,
    )
```

```python
import functools

import jax
import jax.numpy as jnp
from jax import lax
from jax.experimental import pallas as pl
from jax.experimental.pallas import tpu as pltpu
from jax.sharding import PartitionSpec as P

MESH = pl.DeviceIdType.MESH
ROWS = 192
WIN = 144
QUAD = 48
C = 192
HEADS = 6
HD = 32
LAGS = 276
TAB = 3312
SCALE = HD**-0.5
epsilon = 1e-05
f32, bf16 = jnp.float32, jnp.bfloat16


def mm(a, b):
    return lax.dot_general(a, b, (((1,), (0,)), ((), ())), preferred_element_type=f32)


def mm_nt(a, b):
    return lax.dot_general(a, b, (((1,), (1,)), ((), ())), preferred_element_type=f32)


def mm_tn(a, b):
    return lax.dot_general(a, b, (((0,), (0,)), ((), ())), preferred_element_type=f32)


def row_parts(row):
    half = (row >= 96).astype(jnp.int32)
    lon = (row >> 3) - 12 * half
    slot = row & 7
    level = (slot >= 3).astype(jnp.int32)
    return half, lon, slot, level, slot - 3 * level


def iota(shape, dim):
    return lax.broadcasted_iota(jnp.int32, shape, dim)


def to_rows_matrix():
    half, lon, slot, level, lat = row_parts(iota((ROWS, 1), 0))
    source = ((half * 3 + lat) * 12 + lon) * 2 + level
    source = jnp.where(slot < 6, source, -1)
    return (iota((ROWS, WIN), 1) == source).astype(f32).astype(bf16)


def from_rows_matrix():
    half, lon, slot, level, lat = row_parts(iota((1, ROWS), 1))
    target = ((half * 3 + lat) * 12 + lon) * 2 + level
    target = jnp.where(slot < 6, target, -1)
    return (iota((WIN, ROWS), 0) == target).astype(f32).astype(bf16)


def load_grid(ref):
    return ref[...].reshape(WIN, C)


def store_grid(ref, rows):
    ref[...] = rows.astype(bf16).reshape(6, 12, 2, C)


def build_lags(lag_ref):
    half, lon, slot, level, lat = row_parts(iota((ROWS, 1), 0))
    start = (level * 6 + half * 3 + lat) * 23 + lon + 11
    start = jnp.where(slot < 6, start, -100)
    lane = iota((ROWS, LAGS), 1)
    for o in range(12):
        lag_ref[o] = (lane == start - o).astype(f32).astype(bf16)


def table_places(block):
    for half in range(2):
        for slot in range(6):
            level, lat = slot // 3, 3 * half + slot % 3
            levels = [(level, 0), (level, 1)] if block == 0 else [(1 - level, 1), (1 - level, 0)]
            yield half, slot, [((a * 2 + b) * 6 + lat) * 138 for a, b in levels]


def expand(table_ref, flat_ref, lag_ref, bias_ref, block, last):
    flat = table_ref[block].reshape(HEADS, TAB)
    flat_ref[...] = jnp.zeros_like(flat_ref)
    for half, slot, starts in table_places(block):
        pieces = [flat[:, start : start + 138] for start in starts]
        flat_ref[:, half, slot, :] = jnp.concatenate(pieces, axis=1)
    table = flat_ref[...].reshape(96, LAGS)
    high = table.astype(bf16)
    rest = table - high.astype(f32)
    middle = rest.astype(bf16)
    low = (rest - middle.astype(f32)).astype(bf16)
    stacked = jnp.concatenate([high, middle, low], axis=0)
    khalf, _, kslot, klevel, _ = row_parts(iota((1, ROWS), 1))
    key_ok = kslot < 6
    if block:
        row = iota((96, 1), 0)
        slot = row & 7
        qhalf = (row >> 3) & 1
        qlevel = (slot >= 3).astype(jnp.int32)
        same_half = jnp.broadcast_to(qhalf, (96, ROWS)) == jnp.broadcast_to(khalf, (96, ROWS))
        same_level = jnp.broadcast_to(qlevel, (96, ROWS)) == jnp.broadcast_to(klevel, (96, ROWS))
        key_ok = key_ok & same_level & (same_half | jnp.logical_not(last))
    for o in range(12):
        parts = mm_nt(stacked, lag_ref[o])
        full = (parts[:96] + parts[96:192]) + parts[192:]
        full = jnp.where(key_ok, full, -1e30)
        bias_ref[block, :, :, o] = full.reshape(HEADS, 2, 8, ROWS)


def reduce_lags(gs_ref, lag_ref):
    total = jnp.zeros((96, LAGS), f32)
    for o in range(12):
        part = gs_ref[:, :, o].reshape(96, ROWS).astype(bf16)
        total = total + mm(part, lag_ref[o])
    return total


def dense_rows():
    row = iota((1, 96), 1)
    slot = row & 7
    target = (((row >> 3) & 1) * 6 + slot) * 6 + (row >> 4)
    target = jnp.where(slot < 6, target, -1)
    return (iota((80, 96), 0) == target).astype(f32).astype(bf16)


def head_mask(head):
    lane = iota((ROWS, C), 1)
    return (lane >= head * HD) & (lane < (head + 1) * HD)


def only(head, values):
    return jnp.where(head_mask(head), values, jnp.zeros_like(values))


def forward(block, rows_f, gain, w_qkv, w_proj, bias_ref, p_ref):
    centred = rows_f - jnp.mean(rows_f, axis=-1, keepdims=True)
    inv_std = lax.rsqrt(jnp.mean(centred * centred, axis=-1, keepdims=True) + epsilon)
    normed = centred * inv_std
    normed_b = (normed * gain).astype(bf16)
    q = mm(normed_b, w_qkv[:, :C]).astype(bf16)
    k = mm(normed_b, w_qkv[:, C : 2 * C]).astype(bf16)
    v = mm(normed_b, w_qkv[:, 2 * C :]).astype(bf16)
    mixed = jnp.zeros((ROWS, C), f32)
    for head in range(HEADS):
        bias = bias_ref[block, head].reshape(ROWS, ROWS)
        scores = mm_nt(only(head, q), k) * SCALE + bias
        exp_scores = jnp.exp(scores - jnp.max(scores, axis=-1, keepdims=True))
        probs = exp_scores / jnp.sum(exp_scores, axis=-1, keepdims=True)
        p_ref[block, head] = probs
        mixed = jnp.where(head_mask(head), mm(probs.astype(bf16), v), mixed)
    mixed_b = mixed.astype(bf16)
    result = rows_f + mm(mixed_b, w_proj)
    return result, (normed, inv_std, normed_b, q, k, v, mixed_b)


def backward(block, saved, grad_b, gain, w_qkv, w_proj, p_ref, gs_ref):
    normed, inv_std, normed_b, q, k, v, mixed_b = saved
    grad_mixed = mm_nt(grad_b, w_proj).astype(bf16)
    grad_q = jnp.zeros((ROWS, C), f32)
    grad_k = jnp.zeros((ROWS, C), f32)
    grad_v = jnp.zeros((ROWS, C), f32)
    for head in range(HEADS):
        probs = p_ref[block, head]
        grad_head = only(head, grad_mixed)
        grad_probs = mm_nt(grad_head, v)
        weighted = jnp.sum(probs * grad_probs, axis=-1, keepdims=True)
        grad_scores = probs * (grad_probs - weighted)
        gs_ref[head] = grad_scores.reshape(2, 12, 8, ROWS)
        scores_b = grad_scores.astype(bf16)
        grad_q = jnp.where(head_mask(head), mm(scores_b, k), grad_q)
        grad_k = grad_k + mm_tn(scores_b, only(head, q))
        grad_v = grad_v + mm_tn(probs.astype(bf16), grad_head)
    grad_q = (grad_q * SCALE).astype(bf16)
    grad_k = (grad_k * SCALE).astype(bf16)
    grad_v = grad_v.astype(bf16)
    sums = jnp.concatenate(
        [mm_tn(normed_b, grad_q), mm_tn(normed_b, grad_k), mm_tn(normed_b, grad_v)], axis=1
    )
    grad_normed = mm_nt(grad_q, w_qkv[:, :C]) + mm_nt(grad_k, w_qkv[:, C : 2 * C])
    grad_normed = grad_normed + mm_nt(grad_v, w_qkv[:, 2 * C :])
    gain_sum = jnp.sum(grad_normed * normed, axis=0, keepdims=True)
    grad_scaled = grad_normed * gain
    grad_centre = grad_scaled - jnp.mean(grad_scaled, axis=-1, keepdims=True)
    grad_centre = grad_centre - normed * jnp.mean(grad_scaled * normed, axis=-1, keepdims=True)
    grad_in = (grad_b.astype(f32) + inv_std * grad_centre).astype(bf16)
    return grad_in, gain_sum, sums


def place():
    lon, lat = lax.axis_index("lon"), lax.axis_index("lat")
    core, y, low = lax.rem(lon, 2), lax.rem(lax.div(lon, 2), 4), lax.div(lon, 8)
    return dict(core=core, y=y, low=low, high=lax.div(lat, 4), x=lax.rem(lat, 4), lon=lon, lat=lat)


def device(core, y, low, high, x):
    return {"lon": (low * 4 + y) * 2 + core, "lat": high * 4 + x}


class Halo:
    def __init__(self, src, dst, send, recv, towards, sizes):
        self.src, self.dst, self.send, self.recv, self.towards = src, dst, send, recv, towards
        self.sizes = sizes

    def copies(self):
        me = place()
        n_lon, n_lat = self.sizes
        found = []
        for slot, (half, lon_half) in enumerate([(0, 0), (0, 1), (1, 0)]):
            if self.towards < 0:
                lat = lax.rem(me["lat"] - (1 - half) + n_lat, n_lat)
                lon = lax.rem(me["lon"] - (1 - lon_half) + n_lon, n_lon)
                source = (half, lon_half)
            else:
                lat = lax.rem(me["lat"] + 1 - half, n_lat)
                lon = lax.rem(me["lon"] + 1 - lon_half, n_lon)
                source = (1 - half, 1 - lon_half)
            start = source[0] * 96 + source[1] * QUAD
            end = (1 - source[0]) * 96 + (1 - source[1]) * QUAD
            found.append(
                pltpu.make_async_remote_copy(
                    src_ref=self.src.at[pl.ds(start, QUAD)],
                    dst_ref=self.dst.at[pl.ds(end, QUAD)],
                    send_sem=self.send.at[slot],
                    recv_sem=self.recv.at[slot],
                    device_id={"lon": lon, "lat": lat},
                    device_id_type=MESH,
                )
            )
        return found

    def start(self):
        for copy in self.copies():
            copy.start()
        own = 96 + QUAD if self.towards < 0 else 0
        there = 0 if self.towards < 0 else 96 + QUAD
        self.dst[there : there + QUAD] = self.src[own : own + QUAD]

    def finish(self):
        for copy in self.copies():
            copy.wait_recv()

    def drain(self):
        for copy in self.copies():
            copy.wait_send()


NEAR = [(0, dy, dc) for dy in (2, 1, 3, 0) for dc in (1, 0) if (dy, dc) != (0, 0)]
WIDE = [(dx, dy, dc) for dx in (2, 1, 3) for dy in (2, 1, 3, 0) for dc in (1, 0)]
T_ROWS = 32


def piece(index, rows):
    return pl.ds(pl.multiple_of(index * rows, rows), rows)


def weight_lanes(parts, gains):
    rest = [gains[:, 64 * n : 64 * n + 64] for n in range(3)] + [jnp.zeros((ROWS - 3, 64), f32)]
    return jnp.concatenate(parts + [jnp.concatenate(rest, axis=0)], axis=1)


class Sums:
    def __init__(self, refs, send, recv):
        self.w_src, self.t_src, self.w_in, self.t_in, self.along, self.all = refs
        self.rows = self.w_src.shape[1]
        self.send, self.recv = send, recv
        self.me = me = place()
        self.at = (me["y"] * 4 + me["x"]) * 2 + me["core"]
        self.t_at = me["y"] * 2 + me["core"]
        self.z_at = me["high"] * 8 + me["low"]

    def copy(self, step, src, dst, to):
        pltpu.make_async_remote_copy(
            src_ref=src, dst_ref=dst, send_sem=self.send.at[step], recv_sem=self.recv.at[step],
            device_id=to, device_id_type=MESH,
        ).start()

    def total(self, step):
        near = self.all.at[pl.ds(0, len(NEAR))]
        return (self.w_in, self.t_in, near, self.w_in.at[pl.ds(0, 8)], near, self.w_in.at[pl.ds(0, len(WIDE))])[step]

    def wait(self, step):
        pltpu.make_async_copy(self.total(step), self.total(step), self.recv.at[step]).wait()

    def drain(self):
        for step in range(6):
            pltpu.make_async_copy(self.total(step), self.total(step), self.send.at[step]).wait()

    def fill(self, lanes):
        each, tiles = ROWS // self.rows, lanes.shape[1] // 128
        for tile in range(tiles):
            part = lanes[:, tile * 128 : (tile + 1) * 128]
            self.w_src[each * tile : each * tile + each] = part.reshape(each, self.rows, 128).astype(bf16)
        if each * tiles < 32:
            self.w_src[each * tiles :] = jnp.zeros((32 - each * tiles, self.rows, 128), bf16)

    def fill_table(self, table):
        table = jnp.concatenate([table, jnp.zeros((96, 384 - LAGS), f32)], axis=1)
        table = mm(dense_rows(), table.astype(bf16)).astype(bf16)
        for tile in range(3):
            self.t_src[80 * tile : 80 * tile + 80] = table[:, tile * 128 : (tile + 1) * 128]
        self.t_src[240:256] = jnp.zeros((16, 128), bf16)

    def plane(self, dx, dy, dc):
        me = self.me
        x, y, core = lax.rem(me["x"] + dx, 4), lax.rem(me["y"] + dy, 4), lax.rem(me["core"] + dc, 2)
        return (y * 4 + x) * 2 + core, y * 2 + core, device(core, y, me["low"], me["high"], x)

    def scatter(self):
        for slot, offset in enumerate(WIDE + NEAR):
            at, _, to = self.plane(*offset)
            self.copy(0, self.w_src.at[at], self.w_in.at[slot], to)

    def scatter_table(self):
        for slot, offset in enumerate(NEAR):
            _, at, to = self.plane(*offset)
            self.copy(1, self.t_src.at[piece(at, T_ROWS)], self.t_in.at[slot], to)

    def scattered(self):
        self.wait(0)
        total = self.w_src[self.at].astype(f32)
        for slot in range(31):
            total = total + self.w_in[slot].astype(f32)
        self.along[self.z_at, : self.rows] = total.astype(bf16)

    def scattered_table(self):
        self.wait(1)
        total = self.t_src[piece(self.t_at, T_ROWS)].astype(f32)
        for slot in range(len(NEAR)):
            total = total + self.t_in[slot].astype(f32)
        self.along[self.z_at, self.rows :] = total.astype(bf16)

    def line(self, dz, other):
        me = self.me
        high = 1 - me["high"] if other else me["high"]
        return device(me["core"], me["y"], lax.rem(me["low"] + dz, 8), high, me["x"])

    def exchange(self):
        own = self.along.at[self.z_at, pl.ds(0, self.rows)]
        for dz in (0, 1, 7, 2, 6, 3, 5, 4):
            self.copy(3, own, own, self.line(dz, True))

    def exchange_near(self):
        own = self.along.at[self.z_at]
        for dz in (4, 3, 5, 2, 6, 1, 7):
            self.copy(2, own, own, self.line(dz, False))

    def exchanged(self):
        self.wait(2)
        self.wait(3)
        weights = self.along[0, : self.rows].astype(f32)
        for slot in range(1, 16):
            weights = weights + self.along[slot, : self.rows].astype(f32)
        self.all[self.at, : self.rows] = weights.astype(bf16)
        base = self.me["high"] * 8
        table = self.along[base, self.rows :].astype(f32)
        for slot in range(1, 8):
            table = table + self.along[base + slot, self.rows :].astype(f32)
        self.all[self.at, self.rows :] = table.astype(bf16)

    def gather(self):
        own = self.all.at[self.at, pl.ds(0, self.rows)]
        for offset in WIDE:
            self.copy(5, own, own, self.plane(*offset)[2])
        own = self.all.at[self.at]
        for offset in NEAR:
            self.copy(4, own, own, self.plane(*offset)[2])

    def gathered(self, w_ref, t_ref):
        self.wait(4)
        self.wait(5)
        w_ref[...] = self.all[:, : self.rows]
        for y in range(4):
            for core in range(2):
                at = y * 2 + core
                t_ref[at * T_ROWS : at * T_ROWS + T_ROWS] = self.all[(y * 4 + self.me["x"]) * 2 + core, self.rows :]


def finish(scale, table_scale, grid_a, grid_b, w_one, w_two, t_one, t_two,
           out_ref, field_ref, gains_ref, qkv_ref, proj_ref, table_ref, flat_ref):
    out_ref[...] = grid_a[...]
    field_ref[...] = grid_b[...]
    for block, (w_all, t_all, rows, count) in enumerate(((w_one, t_one, 32, 5), (w_two, t_two, 48, 8))):
        each = ROWS // rows
        tiles = [w_all[each * n : each * n + each].astype(f32).reshape(ROWS, 128) * scale for n in range(count)]
        for tile in range(4):
            qkv_ref[block, :, tile * 128 : (tile + 1) * 128] = tiles[tile]
        qkv_ref[block, :, 512:576] = tiles[4][:, :64]
        if block:
            proj_ref[1] = jnp.concatenate([tiles[4][:, 64:], tiles[5]], axis=1)
            proj_ref[0, :, :128] = tiles[6]
            proj_ref[0, :, 128:] = tiles[7][:, :64]
        gains = tiles[-1][:8, 64:]
        gains_ref[block : block + 1] = jnp.concatenate([gains[n : n + 1] for n in range(3)], axis=1)
        parts = [t_all[80 * tile : 80 * tile + 80].astype(f32) for tile in range(3)]
        table = jnp.concatenate(parts, axis=1) * table_scale
        for half, slot, starts in table_places(block):
            row = (half * 6 + slot) * 6
            for index, start in enumerate(starts):
                flat_ref[:, start : start + 138] = table[row : row + 6, index * 138 : index * 138 + 138]
        table_ref[block] = flat_ref[...].reshape(HEADS, 1, TAB)


def kernel(sizes, x_ref, ct_ref, gain_ref, w_qkv_ref, w_proj_ref, table_ref,
           out_ref, field_ref, w_one, w_two, t_one, t_two,
           flat_ref, lag_ref, bias_ref, p_ref, gs_ref, halo_src, halo_dst, halo_send, halo_recv, *sum_refs):
    n_lon, n_lat = sizes
    alone = n_lon * n_lat == 1
    me = place()
    if not alone:
        barrier = pltpu.get_barrier_semaphore()
        count = 0
        for dlat, dlon in ((0, 1), (1, 0), (1, 1)):
            for sign in (1, -1):
                to = {"lon": lax.rem(me["lon"] + sign * dlon + n_lon, n_lon), "lat": lax.rem(me["lat"] + sign * dlat + n_lat, n_lat)}
                pl.semaphore_signal(barrier, inc=1, device_id=to, device_id_type=MESH)
                count += 1
        partners = []
        for dx, dy, dc in WIDE + NEAR:
            x, y, core = lax.rem(me["x"] + dx, 4), lax.rem(me["y"] + dy, 4), lax.rem(me["core"] + dc, 2)
            partners.append(device(core, y, me["low"], me["high"], x))
        for dz in range(8):
            partners.append(device(me["core"], me["y"], lax.rem(me["low"] + dz, 8), 1 - me["high"], me["x"]))
            if dz:
                partners.append(device(me["core"], me["y"], lax.rem(me["low"] + dz, 8), me["high"], me["x"]))
        for to in partners:
            pl.semaphore_signal(barrier, inc=1, device_id=to, device_id_type=MESH)
        count += len(partners)
    halos = [
        Halo(halo_src.at[n], halo_dst.at[n], halo_send.at[n], halo_recv.at[n], 1 if n in (2, 3) else -1, sizes)
        for n in range(5)
    ]
    first, turned, second, back, shared = halos

    def exchange(halo, rows):
        halo.src[...] = rows
        if alone:
            for half in range(2):
                for lon_half in range(2):
                    start = half * 96 + lon_half * QUAD
                    end = (1 - half) * 96 + (1 - lon_half) * QUAD
                    halo.dst[end : end + QUAD] = halo.src[start : start + QUAD]
        else:
            halo.start()

    def arrived(halo):
        if not alone:
            halo.finish()
        return halo.dst[...]

    last = me["lat"] == n_lat - 1
    to_rows = to_rows_matrix()
    from_rows = from_rows_matrix()
    x_rows = mm(to_rows, load_grid(x_ref))
    ct_rows = mm(to_rows, load_grid(ct_ref)).astype(bf16)
    build_lags(lag_ref)
    expand(table_ref, flat_ref, lag_ref, bias_ref, 0, last)
    gain = [gain_ref[0:1], gain_ref[1:2]]
    w_qkv = [w_qkv_ref[0], w_qkv_ref[1]]
    w_proj = [w_proj_ref[0], w_proj_ref[1]]
    first_out, saved_first = forward(0, x_rows, gain[0], w_qkv[0], w_proj[0], bias_ref, p_ref)
    if not alone:
        pl.semaphore_wait(barrier, count)
    exchange(first, first_out.astype(bf16))
    exchange(turned, ct_rows)
    exchange(shared, saved_first[-1])
    expand(table_ref, flat_ref, lag_ref, bias_ref, 1, last)
    shifted = arrived(first).astype(f32)
    second_out, saved_second = forward(1, shifted, gain[1], w_qkv[1], w_proj[1], bias_ref, p_ref)
    exchange(second, second_out.astype(bf16))
    grad_second = arrived(turned)
    grad_shifted, gain_two, sums_two = backward(1, saved_second, grad_second, gain[1], w_qkv[1], w_proj[1], p_ref, gs_ref)
    exchange(back, grad_shifted)
    half = len(sum_refs) // 2
    two = Sums(sum_refs[: half - 2], *sum_refs[half - 2 : half])
    one = Sums(sum_refs[half : 2 * half - 2], *sum_refs[2 * half - 2 :])
    proj_one = mm_tn(arrived(shared), grad_shifted)
    proj_two = mm_tn(saved_second[-1], grad_second)
    two.fill(weight_lanes([sums_two, proj_two, proj_one], gain_two))
    if not alone:
        two.scatter()
    two.fill_table(reduce_lags(gs_ref, lag_ref))
    if not alone:
        two.scatter_table()
    grad_first = arrived(back)
    grad_field, gain_one, sums_one = backward(0, saved_first, grad_first, gain[0], w_qkv[0], w_proj[0], p_ref, gs_ref)
    one.fill(weight_lanes([sums_one], gain_one))
    if alone:
        one.fill_table(reduce_lags(gs_ref, lag_ref))
        for sums, w_ref, t_ref in ((one, w_one, t_one), (two, w_two, t_two)):
            w_ref[...] = sums.w_src[...]
            t_ref[...] = sums.t_src[...]
    else:
        one.scatter()
        two.scattered()
        two.exchange()
        two.scattered_table()
        two.exchange_near()
        one.fill_table(reduce_lags(gs_ref, lag_ref))
        one.scatter_table()
    store_grid(field_ref, mm(from_rows, grad_field))
    store_grid(out_ref, mm(from_rows, arrived(second)))
    if not alone:
        one.scattered()
        one.exchange()
        one.scattered_table()
        one.exchange_near()
        two.exchanged()
        two.gather()
        for halo in halos:
            halo.drain()
        one.exchanged()
        one.gather()
        two.gathered(w_two, t_two)
        two.drain()
        one.gathered(w_one, t_one)
        one.drain()


def per_device(fields, cotangent, norm_gains, w_qkv, w_proj, tables, *, sizes, interpret=False):
    n_lon, n_lat = sizes
    scale = float(2 * 6 * n_lat * 12 * n_lon) ** -0.5
    table_scale = float(n_lon) ** -0.5
    vmem = pl.BlockSpec(memory_space=pltpu.VMEM)
    grid = jax.ShapeDtypeStruct((6, 12, 2, C), bf16)
    w_one, w_two, t_shape = (32, 32, 128), (32, 48, 128), (256, 128)
    many = n_lon * n_lat > 1

    def scratch(w_shape):
        part = w_shape[1] + T_ROWS
        return [
            pltpu.VMEM(w_shape, bf16),
            pltpu.VMEM(t_shape, bf16),
            pltpu.VMEM((31, w_shape[1], 128), bf16),
            pltpu.VMEM((len(NEAR), T_ROWS, 128), bf16),
            pltpu.VMEM((16, part, 128), bf16),
            pltpu.VMEM((32, part, 128), bf16),
            pltpu.SemaphoreType.DMA((6,)),
            pltpu.SemaphoreType.DMA((6,)),
        ]

    found = pl.pallas_call(
        functools.partial(kernel, sizes),
        out_shape=[grid, grid] + [jax.ShapeDtypeStruct(shape, bf16) for shape in (w_one, w_two, t_shape, t_shape)],
        in_specs=[vmem] * 6,
        out_specs=[vmem] * 6,
        scratch_shapes=[
            pltpu.VMEM((HEADS, 2, 8, LAGS), f32),
            pltpu.VMEM((12, ROWS, LAGS), bf16),
            pltpu.VMEM((2, HEADS, 2, 12, 8, ROWS), f32),
            pltpu.VMEM((2, HEADS, ROWS, ROWS), f32),
            pltpu.VMEM((HEADS, 2, 12, 8, ROWS), f32),
            pltpu.VMEM((5, ROWS, C), bf16),
            pltpu.VMEM((5, ROWS, C), bf16),
            pltpu.SemaphoreType.DMA((5, 3)),
            pltpu.SemaphoreType.DMA((5, 3)),
        ]
        + scratch(w_two)
        + scratch(w_one),
        compiler_params=pltpu.CompilerParams(
            collective_id=0 if many else None, has_side_effects=True, vmem_limit_bytes=56 * 2**20
        ),
        interpret=interpret,
    )(
        fields.transpose(1, 2, 0, 3),
        cotangent.transpose(1, 2, 0, 3),
        norm_gains,
        w_qkv,
        w_proj,
        tables.transpose(0, 2, 1, 3),
    )
    outs = pl.pallas_call(
        functools.partial(finish, scale, table_scale),
        out_shape=[
            grid,
            grid,
            jax.ShapeDtypeStruct((2, C), f32),
            jax.ShapeDtypeStruct((2, C, 3 * C), f32),
            jax.ShapeDtypeStruct((2, C, C), f32),
            jax.ShapeDtypeStruct((2, HEADS, 1, TAB), f32),
        ],
        in_specs=[vmem] * 6,
        out_specs=[vmem] * 6,
        scratch_shapes=[pltpu.VMEM((HEADS, TAB), f32)],
        compiler_params=pltpu.CompilerParams(vmem_limit_bytes=60 * 2**20),
        interpret=interpret,
    )(*found)
    grids = [rows.transpose(2, 0, 1, 3) for rows in outs[:2]]
    return (*grids, *outs[2:5], outs[5].transpose(0, 2, 1, 3))


def solution(mesh):
    grid = P(None, "lat", "lon", None)
    bands = P(None, "lat", None, None)
    sizes = (mesh.shape["lon"], mesh.shape["lat"])
    return jax.shard_map(
        functools.partial(per_device, sizes=sizes),
        mesh=mesh,
        in_specs=(grid, grid, P(), P(), P(), bands),
        out_specs=(grid, grid, P(), P(), P(), bands),
        check_vma=False,
    )
```

```python
import functools

import jax
import jax.numpy as jnp
from jax import lax
from jax.experimental import pallas as pl
from jax.experimental.pallas import tpu as pltpu
from jax.sharding import PartitionSpec as P

MESH = pl.DeviceIdType.MESH
ROWS = 192
WIN = 144
QUAD = 48
C = 192
HEADS = 6
HD = 32
LAGS = 276
TAB = 3312
SCALE = HD**-0.5
epsilon = 1e-05
f32, bf16 = jnp.float32, jnp.bfloat16


def mm(a, b):
    return lax.dot_general(a, b, (((1,), (0,)), ((), ())), preferred_element_type=f32)


def mm_nt(a, b):
    return lax.dot_general(a, b, (((1,), (1,)), ((), ())), preferred_element_type=f32)


def mm_tn(a, b):
    return lax.dot_general(a, b, (((0,), (0,)), ((), ())), preferred_element_type=f32)


def row_parts(row):
    half = (row >= 96).astype(jnp.int32)
    lon = (row >> 3) - 12 * half
    slot = row & 7
    level = (slot >= 3).astype(jnp.int32)
    return half, lon, slot, level, slot - 3 * level


def iota(shape, dim):
    return lax.broadcasted_iota(jnp.int32, shape, dim)


def to_rows_matrix():
    half, lon, slot, level, lat = row_parts(iota((ROWS, 1), 0))
    source = ((half * 3 + lat) * 12 + lon) * 2 + level
    source = jnp.where(slot < 6, source, -1)
    return (iota((ROWS, WIN), 1) == source).astype(f32).astype(bf16)


def from_rows_matrix():
    half, lon, slot, level, lat = row_parts(iota((1, ROWS), 1))
    target = ((half * 3 + lat) * 12 + lon) * 2 + level
    target = jnp.where(slot < 6, target, -1)
    return (iota((WIN, ROWS), 0) == target).astype(f32).astype(bf16)


def load_grid(ref):
    return ref[...].reshape(WIN, C)


def store_grid(ref, rows):
    ref[...] = rows.astype(bf16).reshape(6, 12, 2, C)


def build_lags(lag_ref):
    half, lon, slot, level, lat = row_parts(iota((ROWS, 1), 0))
    start = (level * 6 + half * 3 + lat) * 23 + lon + 11
    start = jnp.where(slot < 6, start, -100)
    lane = iota((ROWS, LAGS), 1)
    for o in range(12):
        lag_ref[o] = (lane == start - o).astype(f32).astype(bf16)


def table_places(block):
    for half in range(2):
        for slot in range(6):
            level, lat = slot // 3, 3 * half + slot % 3
            levels = [(level, 0), (level, 1)] if block == 0 else [(1 - level, 1), (1 - level, 0)]
            yield half, slot, [((a * 2 + b) * 6 + lat) * 138 for a, b in levels]


def expand(table_ref, flat_ref, lag_ref, bias_ref, block, last):
    flat = table_ref[block].reshape(HEADS, TAB)
    flat_ref[...] = jnp.zeros_like(flat_ref)
    for half, slot, starts in table_places(block):
        pieces = [flat[:, start : start + 138] for start in starts]
        flat_ref[:, half, slot, :] = jnp.concatenate(pieces, axis=1)
    table = flat_ref[...].reshape(96, LAGS)
    high = table.astype(bf16)
    rest = table - high.astype(f32)
    middle = rest.astype(bf16)
    low = (rest - middle.astype(f32)).astype(bf16)
    stacked = jnp.concatenate([high, middle, low], axis=0)
    khalf, _, kslot, klevel, _ = row_parts(iota((1, ROWS), 1))
    key_ok = kslot < 6
    if block:
        row = iota((96, 1), 0)
        slot = row & 7
        qhalf = (row >> 3) & 1
        qlevel = (slot >= 3).astype(jnp.int32)
        same_half = jnp.broadcast_to(qhalf, (96, ROWS)) == jnp.broadcast_to(khalf, (96, ROWS))
        same_level = jnp.broadcast_to(qlevel, (96, ROWS)) == jnp.broadcast_to(klevel, (96, ROWS))
        key_ok = key_ok & same_level & (same_half | jnp.logical_not(last))
    for o in range(12):
        parts = mm_nt(stacked, lag_ref[o])
        full = (parts[:96] + parts[96:192]) + parts[192:]
        full = jnp.where(key_ok, full, -1e30)
        bias_ref[block, :, :, o] = full.reshape(HEADS, 2, 8, ROWS)


def reduce_lags(gs_ref, lag_ref):
    total = jnp.zeros((96, LAGS), f32)
    for o in range(12):
        part = gs_ref[:, :, o].reshape(96, ROWS).astype(bf16)
        total = total + mm(part, lag_ref[o])
    return total


def dense_rows():
    row = iota((1, 96), 1)
    slot = row & 7
    target = (((row >> 3) & 1) * 6 + slot) * 6 + (row >> 4)
    target = jnp.where(slot < 6, target, -1)
    return (iota((80, 96), 0) == target).astype(f32).astype(bf16)


def head_mask(head):
    lane = iota((ROWS, C), 1)
    return (lane >= head * HD) & (lane < (head + 1) * HD)


def only(head, values):
    return jnp.where(head_mask(head), values, jnp.zeros_like(values))


def forward(block, rows_f, gain, w_qkv, w_proj, bias_ref, p_ref):
    centred = rows_f - jnp.mean(rows_f, axis=-1, keepdims=True)
    inv_std = lax.rsqrt(jnp.mean(centred * centred, axis=-1, keepdims=True) + epsilon)
    normed = centred * inv_std
    normed_b = (normed * gain).astype(bf16)
    q = mm(normed_b, w_qkv[:, :C]).astype(bf16)
    k = mm(normed_b, w_qkv[:, C : 2 * C]).astype(bf16)
    v = mm(normed_b, w_qkv[:, 2 * C :]).astype(bf16)
    mixed = jnp.zeros((ROWS, C), f32)
    for head in range(HEADS):
        bias = bias_ref[block, head].reshape(ROWS, ROWS)
        scores = mm_nt(only(head, q), k) * SCALE + bias
        exp_scores = jnp.exp(scores - jnp.max(scores, axis=-1, keepdims=True))
        probs = exp_scores / jnp.sum(exp_scores, axis=-1, keepdims=True)
        p_ref[block, head] = probs
        mixed = jnp.where(head_mask(head), mm(probs.astype(bf16), v), mixed)
    mixed_b = mixed.astype(bf16)
    result = rows_f + mm(mixed_b, w_proj)
    return result, (normed, inv_std, normed_b, q, k, v, mixed_b)


def backward(block, saved, grad_b, gain, w_qkv, w_proj, p_ref, gs_ref):
    normed, inv_std, normed_b, q, k, v, mixed_b = saved
    grad_mixed = mm_nt(grad_b, w_proj).astype(bf16)
    grad_q = jnp.zeros((ROWS, C), f32)
    grad_k = jnp.zeros((ROWS, C), f32)
    grad_v = jnp.zeros((ROWS, C), f32)
    for head in range(HEADS):
        probs = p_ref[block, head]
        grad_head = only(head, grad_mixed)
        grad_probs = mm_nt(grad_head, v)
        weighted = jnp.sum(probs * grad_probs, axis=-1, keepdims=True)
        grad_scores = probs * (grad_probs - weighted)
        gs_ref[head] = grad_scores.reshape(2, 12, 8, ROWS)
        scores_b = grad_scores.astype(bf16)
        grad_q = jnp.where(head_mask(head), mm(scores_b, k), grad_q)
        grad_k = grad_k + mm_tn(scores_b, only(head, q))
        grad_v = grad_v + mm_tn(probs.astype(bf16), grad_head)
    grad_q = (grad_q * SCALE).astype(bf16)
    grad_k = (grad_k * SCALE).astype(bf16)
    grad_v = grad_v.astype(bf16)
    grad_normed = mm_nt(grad_q, w_qkv[:, :C]) + mm_nt(grad_k, w_qkv[:, C : 2 * C])
    grad_normed = grad_normed + mm_nt(grad_v, w_qkv[:, 2 * C :])
    gain_sum = jnp.sum(grad_normed * normed, axis=0, keepdims=True)

    def weight_sums():
        return jnp.concatenate([mm_tn(normed_b, part) for part in (grad_q, grad_k, grad_v)], axis=1)

    def grad_in():
        grad_scaled = grad_normed * gain
        grad_centre = grad_scaled - jnp.mean(grad_scaled, axis=-1, keepdims=True)
        grad_centre = grad_centre - normed * jnp.mean(grad_scaled * normed, axis=-1, keepdims=True)
        return (grad_b.astype(f32) + inv_std * grad_centre).astype(bf16)

    return grad_in, gain_sum, weight_sums


def place():
    lon, lat = lax.axis_index("lon"), lax.axis_index("lat")
    core, y, low = lax.rem(lon, 2), lax.rem(lax.div(lon, 2), 4), lax.div(lon, 8)
    return dict(core=core, y=y, low=low, high=lax.div(lat, 4), x=lax.rem(lat, 4), lon=lon, lat=lat)


def device(core, y, low, high, x):
    return {"lon": (low * 4 + y) * 2 + core, "lat": high * 4 + x}


class Halo:
    def __init__(self, src, dst, send, recv, towards, sizes):
        self.src, self.dst, self.send, self.recv, self.towards = src, dst, send, recv, towards
        self.sizes = sizes

    def copies(self):
        me = place()
        n_lon, n_lat = self.sizes
        found = []
        for slot, (half, lon_half) in enumerate([(0, 0), (0, 1), (1, 0)]):
            if self.towards < 0:
                lat = lax.rem(me["lat"] - (1 - half) + n_lat, n_lat)
                lon = lax.rem(me["lon"] - (1 - lon_half) + n_lon, n_lon)
                source = (half, lon_half)
            else:
                lat = lax.rem(me["lat"] + 1 - half, n_lat)
                lon = lax.rem(me["lon"] + 1 - lon_half, n_lon)
                source = (1 - half, 1 - lon_half)
            start = source[0] * 96 + source[1] * QUAD
            end = (1 - source[0]) * 96 + (1 - source[1]) * QUAD
            found.append(
                pltpu.make_async_remote_copy(
                    src_ref=self.src.at[pl.ds(start, QUAD)],
                    dst_ref=self.dst.at[pl.ds(end, QUAD)],
                    send_sem=self.send.at[slot],
                    recv_sem=self.recv.at[slot],
                    device_id={"lon": lon, "lat": lat},
                    device_id_type=MESH,
                )
            )
        return found

    def start(self):
        for copy in self.copies():
            copy.start()
        own = 96 + QUAD if self.towards < 0 else 0
        there = 0 if self.towards < 0 else 96 + QUAD
        self.dst[there : there + QUAD] = self.src[own : own + QUAD]

    def finish(self):
        for copy in self.copies():
            copy.wait_recv()

    def drain(self):
        for copy in self.copies():
            copy.wait_send()


NEAR = [(0, dy, dc) for dy in (2, 1, 3, 0) for dc in (1, 0) if (dy, dc) != (0, 0)]
WIDE = [(dx, dy, dc) for dx in (2, 1, 3) for dy in (2, 1, 3, 0) for dc in (1, 0)]
T_ROWS = 32


def piece(index, rows):
    return pl.ds(pl.multiple_of(index * rows, rows), rows)


def weight_lanes(parts, gains):
    rest = [gains[:, 64 * n : 64 * n + 64] for n in range(3)] + [jnp.zeros((ROWS - 3, 64), f32)]
    return jnp.concatenate(parts + [jnp.concatenate(rest, axis=0)], axis=1)


class Sums:
    def __init__(self, refs, send, recv):
        self.w_src, self.t_src, self.w_in, self.t_in, self.along, self.all = refs
        self.rows = self.w_src.shape[1]
        self.send, self.recv = send, recv
        self.me = me = place()
        self.at = (me["y"] * 4 + me["x"]) * 2 + me["core"]
        self.t_at = me["y"] * 2 + me["core"]
        self.z_at = me["high"] * 8 + me["low"]

    def copy(self, step, src, dst, to):
        pltpu.make_async_remote_copy(
            src_ref=src, dst_ref=dst, send_sem=self.send.at[step], recv_sem=self.recv.at[step],
            device_id=to, device_id_type=MESH,
        ).start()

    def total(self, step):
        near = self.all.at[pl.ds(0, len(NEAR))]
        return (self.w_in, self.t_in, near, self.w_in.at[pl.ds(0, 8)], near, self.w_in.at[pl.ds(0, len(WIDE))])[step]

    def wait(self, step):
        pltpu.make_async_copy(self.total(step), self.total(step), self.recv.at[step]).wait()

    def drain(self):
        for step in range(6):
            pltpu.make_async_copy(self.total(step), self.total(step), self.send.at[step]).wait()

    def fill(self, lanes):
        each, tiles = ROWS // self.rows, lanes.shape[1] // 128
        for tile in range(tiles):
            part = lanes[:, tile * 128 : (tile + 1) * 128]
            self.w_src[each * tile : each * tile + each] = part.reshape(each, self.rows, 128).astype(bf16)
        if each * tiles < 32:
            self.w_src[each * tiles :] = jnp.zeros((32 - each * tiles, self.rows, 128), bf16)

    def fill_table(self, table):
        table = jnp.concatenate([table, jnp.zeros((96, 384 - LAGS), f32)], axis=1)
        table = mm(dense_rows(), table.astype(bf16)).astype(bf16)
        for tile in range(3):
            self.t_src[80 * tile : 80 * tile + 80] = table[:, tile * 128 : (tile + 1) * 128]
        self.t_src[240:256] = jnp.zeros((16, 128), bf16)

    def plane(self, dx, dy, dc):
        me = self.me
        x, y, core = lax.rem(me["x"] + dx, 4), lax.rem(me["y"] + dy, 4), lax.rem(me["core"] + dc, 2)
        return (y * 4 + x) * 2 + core, y * 2 + core, device(core, y, me["low"], me["high"], x)

    def scatter(self):
        for slot, offset in enumerate(WIDE + NEAR):
            at, _, to = self.plane(*offset)
            self.copy(0, self.w_src.at[at], self.w_in.at[slot], to)

    def scatter_table(self):
        for slot, offset in enumerate(NEAR):
            _, at, to = self.plane(*offset)
            self.copy(1, self.t_src.at[piece(at, T_ROWS)], self.t_in.at[slot], to)

    def scattered(self):
        self.wait(0)
        total = self.w_src[self.at].astype(f32)
        for slot in range(31):
            total = total + self.w_in[slot].astype(f32)
        self.along[self.z_at, : self.rows] = total.astype(bf16)

    def scattered_table(self):
        self.wait(1)
        total = self.t_src[piece(self.t_at, T_ROWS)].astype(f32)
        for slot in range(len(NEAR)):
            total = total + self.t_in[slot].astype(f32)
        self.along[self.z_at, self.rows :] = total.astype(bf16)

    def line(self, dz, other):
        me = self.me
        high = 1 - me["high"] if other else me["high"]
        return device(me["core"], me["y"], lax.rem(me["low"] + dz, 8), high, me["x"])

    def exchange(self):
        own = self.along.at[self.z_at, pl.ds(0, self.rows)]
        for dz in (0, 1, 7, 2, 6, 3, 5, 4):
            self.copy(3, own, own, self.line(dz, True))

    def exchange_near(self):
        own = self.along.at[self.z_at]
        for dz in (4, 3, 5, 2, 6, 1, 7):
            self.copy(2, own, own, self.line(dz, False))

    def exchanged(self):
        self.wait(2)
        self.wait(3)
        weights = self.along[0, : self.rows].astype(f32)
        for slot in range(1, 16):
            weights = weights + self.along[slot, : self.rows].astype(f32)
        self.all[self.at, : self.rows] = weights.astype(bf16)
        base = self.me["high"] * 8
        table = self.along[base, self.rows :].astype(f32)
        for slot in range(1, 8):
            table = table + self.along[base + slot, self.rows :].astype(f32)
        self.all[self.at, self.rows :] = table.astype(bf16)

    def gather(self):
        own = self.all.at[self.at, pl.ds(0, self.rows)]
        for offset in WIDE:
            self.copy(5, own, own, self.plane(*offset)[2])
        own = self.all.at[self.at]
        for offset in NEAR:
            self.copy(4, own, own, self.plane(*offset)[2])

    def gathered(self, w_ref, t_ref):
        self.wait(4)
        self.wait(5)
        w_ref[...] = self.all[:, : self.rows]
        for y in range(4):
            for core in range(2):
                at = y * 2 + core
                t_ref[at * T_ROWS : at * T_ROWS + T_ROWS] = self.all[(y * 4 + self.me["x"]) * 2 + core, self.rows :]


def finish(scale, table_scale, grid_a, grid_b, w_one, w_two, t_one, t_two,
           out_ref, field_ref, gains_ref, qkv_ref, proj_ref, table_ref, flat_ref):
    out_ref[...] = grid_a[...]
    field_ref[...] = grid_b[...]
    for block, (w_all, t_all, rows, count) in enumerate(((w_one, t_one, 32, 5), (w_two, t_two, 48, 8))):
        each = ROWS // rows
        tiles = [w_all[each * n : each * n + each].astype(f32).reshape(ROWS, 128) * scale for n in range(count)]
        for tile in range(4):
            qkv_ref[block, :, tile * 128 : (tile + 1) * 128] = tiles[tile]
        qkv_ref[block, :, 512:576] = tiles[4][:, :64]
        if block:
            proj_ref[1] = jnp.concatenate([tiles[4][:, 64:], tiles[5]], axis=1)
            proj_ref[0, :, :128] = tiles[6]
            proj_ref[0, :, 128:] = tiles[7][:, :64]
        gains = tiles[-1][:8, 64:]
        gains_ref[block : block + 1] = jnp.concatenate([gains[n : n + 1] for n in range(3)], axis=1)
        parts = [t_all[80 * tile : 80 * tile + 80].astype(f32) for tile in range(3)]
        table = jnp.concatenate(parts, axis=1) * table_scale
        for half, slot, starts in table_places(block):
            row = (half * 6 + slot) * 6
            for index, start in enumerate(starts):
                flat_ref[:, start : start + 138] = table[row : row + 6, index * 138 : index * 138 + 138]
        table_ref[block] = flat_ref[...].reshape(HEADS, 1, TAB)


def kernel(sizes, x_ref, ct_ref, gain_ref, w_qkv_ref, w_proj_ref, table_ref,
           out_ref, field_ref, w_one, w_two, t_one, t_two,
           flat_ref, lag_ref, bias_ref, p_ref, gs_ref, halo_src, halo_dst, halo_send, halo_recv, *sum_refs):
    n_lon, n_lat = sizes
    alone = n_lon * n_lat == 1
    me = place()
    if not alone:
        barrier = pltpu.get_barrier_semaphore()
        count = 0
        for dlat, dlon in ((0, 1), (1, 0), (1, 1)):
            for sign in (1, -1):
                to = {"lon": lax.rem(me["lon"] + sign * dlon + n_lon, n_lon), "lat": lax.rem(me["lat"] + sign * dlat + n_lat, n_lat)}
                pl.semaphore_signal(barrier, inc=1, device_id=to, device_id_type=MESH)
                count += 1
        partners = []
        for dx, dy, dc in WIDE + NEAR:
            x, y, core = lax.rem(me["x"] + dx, 4), lax.rem(me["y"] + dy, 4), lax.rem(me["core"] + dc, 2)
            partners.append(device(core, y, me["low"], me["high"], x))
        for dz in range(8):
            partners.append(device(me["core"], me["y"], lax.rem(me["low"] + dz, 8), 1 - me["high"], me["x"]))
            if dz:
                partners.append(device(me["core"], me["y"], lax.rem(me["low"] + dz, 8), me["high"], me["x"]))
        for to in partners:
            pl.semaphore_signal(barrier, inc=1, device_id=to, device_id_type=MESH)
        count += len(partners)
    halos = [
        Halo(halo_src.at[n], halo_dst.at[n], halo_send.at[n], halo_recv.at[n], 1 if n in (2, 3) else -1, sizes)
        for n in range(5)
    ]
    first, turned, second, back, shared = halos

    def exchange(halo, rows):
        halo.src[...] = rows
        if alone:
            for half in range(2):
                for lon_half in range(2):
                    start = half * 96 + lon_half * QUAD
                    end = (1 - half) * 96 + (1 - lon_half) * QUAD
                    halo.dst[end : end + QUAD] = halo.src[start : start + QUAD]
        else:
            halo.start()

    def arrived(halo):
        if not alone:
            halo.finish()
        return halo.dst[...]

    last = me["lat"] == n_lat - 1
    to_rows = to_rows_matrix()
    from_rows = from_rows_matrix()
    x_rows = mm(to_rows, load_grid(x_ref))
    ct_rows = mm(to_rows, load_grid(ct_ref)).astype(bf16)
    build_lags(lag_ref)
    expand(table_ref, flat_ref, lag_ref, bias_ref, 0, last)
    gain = [gain_ref[0:1], gain_ref[1:2]]
    w_qkv = [w_qkv_ref[0], w_qkv_ref[1]]
    w_proj = [w_proj_ref[0], w_proj_ref[1]]
    first_out, saved_first = forward(0, x_rows, gain[0], w_qkv[0], w_proj[0], bias_ref, p_ref)
    if not alone:
        pl.semaphore_wait(barrier, count)
    exchange(first, first_out.astype(bf16))
    exchange(turned, ct_rows)
    exchange(shared, saved_first[-1])
    expand(table_ref, flat_ref, lag_ref, bias_ref, 1, last)
    shifted = arrived(first).astype(f32)
    second_out, saved_second = forward(1, shifted, gain[1], w_qkv[1], w_proj[1], bias_ref, p_ref)
    exchange(second, second_out.astype(bf16))
    grad_second = arrived(turned)
    grad_in, gain_two, weight_sums = backward(1, saved_second, grad_second, gain[1], w_qkv[1], w_proj[1], p_ref, gs_ref)
    grad_shifted = grad_in()
    exchange(back, grad_shifted)
    sums_two = weight_sums()
    half = len(sum_refs) // 2
    two = Sums(sum_refs[: half - 2], *sum_refs[half - 2 : half])
    one = Sums(sum_refs[half : 2 * half - 2], *sum_refs[2 * half - 2 :])
    proj_one = mm_tn(arrived(shared), grad_shifted)
    proj_two = mm_tn(saved_second[-1], grad_second)
    two.fill(weight_lanes([sums_two, proj_two, proj_one], gain_two))
    if not alone:
        two.scatter()
    two.fill_table(reduce_lags(gs_ref, lag_ref))
    if not alone:
        two.scatter_table()
        two.scattered()
        two.exchange()
        two.scattered_table()
        two.exchange_near()
    grad_first = arrived(back)
    grad_in, gain_one, weight_sums = backward(0, saved_first, grad_first, gain[0], w_qkv[0], w_proj[0], p_ref, gs_ref)
    one.fill(weight_lanes([weight_sums()], gain_one))
    if alone:
        one.fill_table(reduce_lags(gs_ref, lag_ref))
        for sums, w_ref, t_ref in ((one, w_one, t_one), (two, w_two, t_two)):
            w_ref[...] = sums.w_src[...]
            t_ref[...] = sums.t_src[...]
    else:
        one.scatter()
        one.fill_table(reduce_lags(gs_ref, lag_ref))
        one.scatter_table()
    store_grid(field_ref, mm(from_rows, grad_in()))
    store_grid(out_ref, mm(from_rows, arrived(second)))
    if not alone:
        one.scattered()
        one.exchange()
        one.scattered_table()
        one.exchange_near()
        two.exchanged()
        two.gather()
        for halo in halos:
            halo.drain()
        one.exchanged()
        one.gather()
        two.gathered(w_two, t_two)
        two.drain()
        one.gathered(w_one, t_one)
        one.drain()


def per_device(fields, cotangent, norm_gains, w_qkv, w_proj, tables, *, sizes, interpret=False):
    n_lon, n_lat = sizes
    scale = float(2 * 6 * n_lat * 12 * n_lon) ** -0.5
    table_scale = float(n_lon) ** -0.5
    vmem = pl.BlockSpec(memory_space=pltpu.VMEM)
    grid = jax.ShapeDtypeStruct((6, 12, 2, C), bf16)
    w_one, w_two, t_shape = (32, 32, 128), (32, 48, 128), (256, 128)
    many = n_lon * n_lat > 1

    def scratch(w_shape):
        part = w_shape[1] + T_ROWS
        return [
            pltpu.VMEM(w_shape, bf16),
            pltpu.VMEM(t_shape, bf16),
            pltpu.VMEM((31, w_shape[1], 128), bf16),
            pltpu.VMEM((len(NEAR), T_ROWS, 128), bf16),
            pltpu.VMEM((16, part, 128), bf16),
            pltpu.VMEM((32, part, 128), bf16),
            pltpu.SemaphoreType.DMA((6,)),
            pltpu.SemaphoreType.DMA((6,)),
        ]

    found = pl.pallas_call(
        functools.partial(kernel, sizes),
        out_shape=[grid, grid] + [jax.ShapeDtypeStruct(shape, bf16) for shape in (w_one, w_two, t_shape, t_shape)],
        in_specs=[vmem] * 6,
        out_specs=[vmem] * 6,
        scratch_shapes=[
            pltpu.VMEM((HEADS, 2, 8, LAGS), f32),
            pltpu.VMEM((12, ROWS, LAGS), bf16),
            pltpu.VMEM((2, HEADS, 2, 12, 8, ROWS), f32),
            pltpu.VMEM((2, HEADS, ROWS, ROWS), f32),
            pltpu.VMEM((HEADS, 2, 12, 8, ROWS), f32),
            pltpu.VMEM((5, ROWS, C), bf16),
            pltpu.VMEM((5, ROWS, C), bf16),
            pltpu.SemaphoreType.DMA((5, 3)),
            pltpu.SemaphoreType.DMA((5, 3)),
        ]
        + scratch(w_two)
        + scratch(w_one),
        compiler_params=pltpu.CompilerParams(
            collective_id=0 if many else None, has_side_effects=True, vmem_limit_bytes=56 * 2**20
        ),
        interpret=interpret,
    )(
        fields.transpose(1, 2, 0, 3),
        cotangent.transpose(1, 2, 0, 3),
        norm_gains,
        w_qkv,
        w_proj,
        tables.transpose(0, 2, 1, 3),
    )
    outs = pl.pallas_call(
        functools.partial(finish, scale, table_scale),
        out_shape=[
            grid,
            grid,
            jax.ShapeDtypeStruct((2, C), f32),
            jax.ShapeDtypeStruct((2, C, 3 * C), f32),
            jax.ShapeDtypeStruct((2, C, C), f32),
            jax.ShapeDtypeStruct((2, HEADS, 1, TAB), f32),
        ],
        in_specs=[vmem] * 6,
        out_specs=[vmem] * 6,
        scratch_shapes=[pltpu.VMEM((HEADS, TAB), f32)],
        compiler_params=pltpu.CompilerParams(vmem_limit_bytes=60 * 2**20),
        interpret=interpret,
    )(*found)
    grids = [rows.transpose(2, 0, 1, 3) for rows in outs[:2]]
    return (*grids, *outs[2:5], outs[5].transpose(0, 2, 1, 3))


def solution(mesh):
    grid = P(None, "lat", "lon", None)
    bands = P(None, "lat", None, None)
    sizes = (mesh.shape["lon"], mesh.shape["lat"])
    return jax.shard_map(
        functools.partial(per_device, sizes=sizes),
        mesh=mesh,
        in_specs=(grid, grid, P(), P(), P(), bands),
        out_specs=(grid, grid, P(), P(), P(), bands),
        check_vma=False,
    )
```
